1024 devices in a mesh: gx: 8 (over x, y_lo), gy: 4 (over y_hi), gz: 32 (over z, core).
Axes of the slice: x: 4, y: 8 (y_hi: 4, y_lo: 2; y = y_hi * 2 + y_lo), z: 16, core: 2. Of those that a mesh axis runs over, the one named last changes fastest.
Arguments:
- positions: float32 [3, 8, 8, 64, 128], P(None, 'gx', 'gy', 'gz'), may hold values from 0 to 1
- velocities: float32 [3, 8, 8, 64, 128], P(None, 'gx', 'gy', 'gz'), may hold values from -1.8 to 1.8
- species: int32 [8, 8, 64, 128], P('gx', 'gy', 'gz'), may hold values from 0 to 1
- counts: int32 [8, 8, 64], P('gx', 'gy', 'gz'), may hold values from 32 to 128
Outputs:
- new_positions: float32 [3, 8, 8, 64, 128], P(None, 'gx', 'gy', 'gz')
- new_velocities: float32 [3, 8, 8, 64, 128], P(None, 'gx', 'gy', 'gz')
The draws below stay inside these ranges and needn't reach their ends.
All inputs are finite; a program needn't handle non-finite values.
Results may differ from the reference program's by a relative error of at most 0.0003.
Values sent between devices are 32-bit elements; how exact they have to be, the bound alone decides.
A program may use at most 32 MiB of HBM per device.

```python
from functools import partial
import jax
import jax.numpy as jnp
from jax import lax

SLOTS = 128
NCX = 8
NCY = 8
NCZ = 64


def plant(entries, stream_key, low, top_value):
    place = [jax.random.randint(jax.random.fold_in(stream_key, axis), (), 0, length) for axis, length in enumerate(entries.shape)]
    longest = entries.shape.index(max(entries.shape))
    neighbour = place[:longest] + [(place[longest] + 1) % entries.shape[longest]] + place[longest + 1:]
    return entries.at[tuple(place)].set(low).at[tuple(neighbour)].set(top_value)


def shard_levels(key, extent, shards, smallest, top_value):
    level = 1.0
    for dim, parts in shards:
        draws = jax.random.uniform(jax.random.fold_in(jax.random.fold_in(key, 6), dim), (parts,), jnp.float32, smallest / len(shards), top_value / len(shards))
        level = level * jnp.repeat(jnp.exp(draws), extent[dim] // parts).reshape((-1,) + (1,) * (len(extent) - 1 - dim))
    return level


def scatter_about(rng, dims, deviation, bound, pieces=(), kind=jnp.bfloat16):
    factor_of = shard_levels(rng, dims, pieces, -0.22, 0.18) if pieces else 1.0
    array = jax.random.normal(rng, dims, jnp.float32) * deviation * factor_of
    return jnp.minimum(jnp.maximum(array, -bound), bound).astype(kind)


def setup_inputs(seed: int = 0) -> dict:
    key_of = jax.random.split(jax.random.key(seed), 5)
    positions = jnp.clip(1.0 * jax.random.uniform(key_of[0], (3, NCX, NCY, NCZ, SLOTS), jnp.float32) ** shard_levels(key_of[0], (3, NCX, NCY, NCZ, SLOTS), ((1, 8), (2, 4), (3, 32)), -0.2, 0.2), 0.0, 1.0)
    velocities = scatter_about(key_of[1], (3, NCX, NCY, NCZ, SLOTS), 0.3, 1.8, ((1, 8), (2, 4), (3, 32)), jnp.float32)
    species = plant(jax.random.randint(key_of[2], (NCX, NCY, NCZ, SLOTS), 0, 2), jax.random.fold_in(key_of[2], 1), 0, 1).astype(jnp.int32)
    counts = plant(jax.random.randint(key_of[3], (NCX, NCY, NCZ), SLOTS // 4, SLOTS + 1), jax.random.fold_in(key_of[3], 1), SLOTS // 4, SLOTS).astype(jnp.int32)
    return {"positions": positions, "velocities": velocities, "species": species, "counts": counts}


time_step = 0.05
neighbour_offsets = [(first_step, second_step, third_step) for first_step in (-1, 0, 1) for second_step in (-1, 0, 1) for third_step in (-1, 0, 1)]

def coefficient(species, first, second):
    return jnp.where(species == 1, second, first).astype(jnp.float32)

def atom_records(species, counts):
    slot_index = lax.broadcasted_iota(jnp.int32, species.shape, 3)
    present = (slot_index < counts[..., None]).astype(jnp.float32)
    amplitude = coefficient(species, 1.0, 1.3) * present
    strength = coefficient(species, 0.3, 0.4) * present
    return (jnp.stack([amplitude, strength], axis=0), present)

def pair_geometry(owned, partner, offset):
    deltas = [partner[component][..., None, :] + float(offset[component]) - owned[component][..., :, None] for component in range(3)]
    square = deltas[0] * deltas[0] + deltas[1] * deltas[1] + deltas[2] * deltas[2]
    smooth = jnp.maximum(1.0 - square, 0.0)
    return (deltas, smooth)

def density_block(owned, partner, offset):
    deltas, smooth = pair_geometry(owned, partner, offset)
    contrib = partner[3][..., None, :] * smooth * smooth * smooth
    if offset == (0, 0, 0):
        slot_count = owned.shape[-1]
        contrib = contrib * (1.0 - jnp.eye(slot_count, dtype=jnp.float32))
    return lax.optimization_barrier(jnp.sum(contrib, axis=-1))

def force_block(owned, partner, slopes, partner_slopes, offset):
    deltas, smooth = pair_geometry(owned, partner, offset)
    weight = 3.0 * smooth * smooth * (slopes[..., :, None] * partner[3][..., None, :] + partner_slopes[..., None, :] * owned[3][..., :, None])
    weight = weight + 2.0 * owned[4][..., :, None] * partner[4][..., None, :] * smooth
    return jnp.stack([-2.0 * lax.optimization_barrier(jnp.sum(weight * deltas[component], axis=-1)) for component in range(3)], axis=0)

def plane_density(paired, offset):
    return density_block(paired[0], paired[1], offset)

def plane_force(paired, offset):
    return force_block(paired[0], paired[1], paired[2], paired[3], offset)

def density_field(atom_pack):
    density = jnp.zeros(atom_pack.shape[1:], jnp.float32)
    for offset in neighbour_offsets:
        partner = jnp.roll(atom_pack, (-offset[0], -offset[1], -offset[2]), axis=(1, 2, 3))
        portion = lax.map(partial(plane_density, offset=offset), (jnp.moveaxis(atom_pack, 1, 0), jnp.moveaxis(partner, 1, 0)))
        density = density + portion
    return density

def force_field(atom_pack, slopes):
    forces = jnp.zeros((3,) + atom_pack.shape[1:], jnp.float32)
    for offset in neighbour_offsets:
        partner = jnp.roll(atom_pack, (-offset[0], -offset[1], -offset[2]), axis=(1, 2, 3))
        partner_slopes = jnp.roll(slopes, (-offset[0], -offset[1], -offset[2]), axis=(0, 1, 2))
        portion = lax.map(partial(plane_force, offset=offset), (jnp.moveaxis(atom_pack, 1, 0), jnp.moveaxis(partner, 1, 0), slopes, partner_slopes))
        forces = forces + jnp.moveaxis(portion, 0, 1)
    return forces

def reference(positions, velocities, species, counts):
    records, present = atom_records(species, counts)
    inverse_mass = coefficient(species, 1.0, 1.6)

    def compute_forces(location):
        atom_pack = jnp.concatenate([location, records], axis=0)
        density = density_field(atom_pack)
        slopes = -0.5 * present / jnp.sqrt(density + 1.0)
        return force_field(atom_pack, slopes)
    location = positions
    velocity = velocities
    forces = compute_forces(location)
    for sweep in range(2):
        velocity = velocity + 0.5 * time_step * inverse_mass * forces
        location = location + time_step * velocity
        forces = compute_forces(location)
        velocity = velocity + 0.5 * time_step * inverse_mass * forces
    return (location, velocity)
```

```python
import functools
import itertools

import jax
import jax.numpy as jnp
from jax import lax
from jax.experimental import pallas as pl
from jax.experimental.pallas import tpu as pltpu
from jax.sharding import PartitionSpec as P

MESH = pl.DeviceIdType.MESH
time_step = 0.05
AXES = ("gx", "gy", "gz")
SOURCE = {0: (1, 2), 1: (2, 1), -1: (1, 1)}
TARGET = {0: 1, 1: 0, -1: 3}
DIRECTIONS = sorted(
    (d for d in itertools.product((-1, 0, 1), repeat=3) if d != (0, 0, 0)),
    key=lambda d: -(4 * abs(d[0] * d[1]) + 2 * abs(d[0]) + 2 * abs(d[1]) + abs(d[2])),
)
f32, bf16 = jnp.float32, jnp.bfloat16


def group_of(d):
    return 0 if d[0] == 0 else (1 if d[1] == 0 else 2)


def group_ref(buffer, group):
    return buffer.at[1, pl.ds(0, 3)] if group == 0 else buffer.at[0]


def group_cell(group, index):
    if group == 0:
        return 1, index
    if group == 1:
        return 2 * (index // 2), 1 + index % 2
    return 2 * (index // 2), 3 * (index % 2)


def pieces(value):
    high = value.astype(bf16).astype(f32)
    rest = value - high
    middle = rest.astype(bf16).astype(f32)
    return high, middle, rest - middle


def strength_of(amplitude):
    return jnp.where(amplitude > 1.15, 0.4, jnp.where(amplitude > 0.0, 0.3, 0.0)).astype(f32)


def kernel(
    pos_ref, vel_ref, spec_ref, count_ref, out_pos, out_vel,
    ext, slo, part, rows, reach, lhs, own, acc, total, vel,
    pos_send, pos_recv, slo_send, slo_recv,
):
    place = [lax.axis_index(a) for a in AXES]
    sizes = [lax.axis_size(a) for a in AXES]

    def device(d):
        return tuple(lax.rem(m + k + s, k) for m, k, s in zip(place, sizes, d))

    barrier = pltpu.get_barrier_semaphore()
    for d in DIRECTIONS:
        pl.semaphore_signal(barrier, inc=1, device_id=device(d), device_id_type=MESH)

    row4 = lax.broadcasted_iota(jnp.int32, (4, 128), 0)
    slot = lax.broadcasted_iota(jnp.int32, (1, 128), 1)
    cells = [(y, z) for y in range(2) for z in range(2)]
    for y, z in cells:
        c = 2 * y + z
        present = slot < count_ref[y, z]
        species = spec_ref[y, pl.ds(z, 1)]
        amplitude = jnp.where(present, jnp.where(species == 1, 1.3, 1.0), 0.0).astype(f32)
        inverse_mass = jnp.where(species == 1, 1.6, 1.0).astype(f32)
        ext[0, 1, 1 + y, 1 + z] = jnp.concatenate([pos_ref[k, y, pl.ds(z, 1)] for k in range(3)] + [amplitude], axis=0)
        vel[c] = jnp.concatenate([vel_ref[k, y, pl.ds(z, 1)] for k in range(3)] + [inverse_mass], axis=0)

    pl.semaphore_wait(barrier, len(DIRECTIONS))

    def send(buffer, e, send_sem, recv_sem):
        for d in DIRECTIONS:
            dx, dy, dz = d
            (sy, ny), (sz, nz) = SOURCE[dy], SOURCE[dz]
            pltpu.make_async_remote_copy(
                src_ref=buffer.at[e, 1, pl.ds(sy, ny), pl.ds(sz, nz)],
                dst_ref=buffer.at[e, 1 - dx, pl.ds(TARGET[dy], ny), pl.ds(TARGET[dz], nz)],
                send_sem=send_sem.at[e, group_of(d)],
                recv_sem=recv_sem.at[e, group_of(d)],
                device_id=device(d),
                device_id_type=MESH,
            ).start()

    def wait(buffer, e, sem, group):
        ref = group_ref(buffer.at[e], group)
        pltpu.make_async_copy(ref, ref, sem.at[e, group]).wait()

    def shift_of(ix, iy, iz):
        fx, fy = (jnp.asarray(v, jnp.int32).astype(f32) for v in (ix, iy))
        return jnp.where(row4 == 0, fx - 1.5, jnp.where(row4 == 1, fy - 2.0, float(iz - 2)))

    def prepare(e, group):
        def one(index, carry):
            ix, iy = group_cell(group, index)
            line = 4 * ix + iy
            for iz in range(4):
                lanes = pl.ds(128 * iz, 128)
                tile = ext[e, ix, iy, iz]
                place_ = tile + shift_of(ix, iy, iz)
                square = jnp.sum(jnp.where(row4 < 3, place_ * place_, 0.0), axis=0, keepdims=True)
                h, m, l = pieces(jnp.where(row4 < 3, place_, square))
                one_ = jnp.ones_like(h)
                zero = jnp.zeros_like(h)
                part[line, :, lanes] = jnp.concatenate([h, m, h, m, l, h, one_, zero], axis=0).astype(bf16)
                reach[line, :, lanes] = jnp.concatenate(
                    [jnp.where(row4 < 3, h, 1.0), jnp.where(row4 < 3, m, 0.0), jnp.where(row4 < 3, l, 0.0), zero], axis=0
                ).astype(bf16)
                amplitude = tile[3:4]
                rows[line, 0:1, lanes] = amplitude
                rows[line, 1:2, lanes] = 3.0 * amplitude
                rows[line, 2:3, lanes] = 2.0 * strength_of(amplitude)
            return carry

        lax.fori_loop(0, 4, one, 0)

    def strips(group, body):
        count = (3, 4, 2)[group]

        def one(index, carry):
            y, k = index // count, index % count
            if group == 0:
                line = 4 + y + k
            elif group == 1:
                line = 8 * (k // 2) + 1 + k % 2
            else:
                line = 8 * k + 3 * y
            for z in range(2):
                body(2 * y + z, line, pl.ds(128 * z, 384))
            return carry

        lax.fori_loop(0, 2 * count, one, 0)

    def smooth(c, line, lanes):
        t = jnp.dot(lhs[c], part[line, :, lanes], preferred_element_type=f32)
        return jnp.maximum(t, 0.0)

    def density_strip(c, line, lanes):
        s = smooth(c, line, lanes)
        u = s * s * s * rows[line, 0:1, lanes]
        acc[c] += u[:, :128] + u[:, 128:256] + u[:, 256:]

    def force_strip(c, line, lanes):
        s = smooth(c, line, lanes)
        wide = lambda q: jnp.concatenate([own[c, q]] * 3, axis=1)
        pull = wide(0) * rows[line, 1:2, lanes] + wide(1) * rows[line, 3:4, lanes]
        w = s * (s * pull + wide(2) * rows[line, 2:3, lanes])
        high = w.astype(bf16)
        low = (w - high.astype(f32)).astype(bf16)
        across = (((1,), (1,)), ((), ()))
        g = reach[line, :, lanes]
        total[c] += lax.dot_general(high, g, across, preferred_element_type=f32) + lax.dot_general(
            low, g, across, preferred_element_type=f32
        )

    def across_rows(value):
        return jnp.transpose(jnp.broadcast_to(value, (128, 128)))

    def evaluate(e, carry):
        send(ext, e, pos_send, pos_recv)
        for y, z in cells:
            c = 2 * y + z
            place_ = ext[e, 1, 1 + y, 1 + z] + shift_of(1, 1 + y, 1 + z)
            square = jnp.sum(jnp.where(row4 < 3, place_ * place_, 0.0), axis=0, keepdims=True)
            h, m, l = pieces(2.0 * place_)
            th, tm, tl = pieces(1.0 - square)
            last = lambda v, fill: jnp.where(row4 < 3, v, fill)
            ends = jnp.where(row4 == 0, th, jnp.where(row4 == 1, tm, jnp.where(row4 == 2, tl, 0.0)))
            side = jnp.concatenate(
                [last(h, -1.0), last(h, -1.0), last(m, 0.0), last(m, 0.0), last(h, -1.0), last(l, 0.0), ends, jnp.zeros_like(h)],
                axis=0,
            )
            lhs[c] = jnp.transpose(side).astype(bf16)
            acc[c] = jnp.zeros((128, 128), f32)
            total[c] = jnp.zeros((128, 16), f32)
            amplitude = ext[e, 1, 1 + y, 1 + z][3:4]
            own[c, 1] = across_rows(amplitude)
            own[c, 2] = across_rows(strength_of(amplitude))
        for group in range(3):
            wait(ext, e, pos_recv, group)
            prepare(e, group)
            strips(group, density_strip)
        for y, z in cells:
            c = 2 * y + z
            amplitude = ext[e, 1, 1 + y, 1 + z][3:4]
            level = jnp.sum(jnp.transpose(acc[c]), axis=0, keepdims=True) - amplitude + 1.0
            slo[e, 1, 1 + y, 1 + z] = jnp.where(amplitude > 0.0, -0.5, 0.0) / jnp.sqrt(level)
        send(slo, e, slo_send, slo_recv)
        for y, z in cells:
            own[2 * y + z, 0] = across_rows(slo[e, 1, 1 + y, 1 + z])
        for group in range(3):
            wait(slo, e, slo_recv, group)

            def spread(index, carry):
                ix, iy = group_cell(group, index)
                for iz in range(4):
                    rows[4 * ix + iy, 3:4, pl.ds(128 * iz, 128)] = 3.0 * slo[e, ix, iy, iz]
                return carry

            lax.fori_loop(0, 4, spread, 0)
            strips(group, force_strip)
        kick = jnp.where(e == 1, 2.0, 1.0) * (0.5 * time_step)
        for y, z in cells:
            c = 2 * y + z
            tile = ext[e, 1, 1 + y, 1 + z]
            place_ = tile + shift_of(1, 1 + y, 1 + z)
            r = jnp.transpose(total[c])
            r = r[0:4] + r[4:8] + r[8:12]
            force = -2.0 * (r - place_ * r[3:4])
            v = vel[c]
            v = jnp.where(row4 < 3, v + kick * v[3:4] * force, v)
            vel[c] = v
            ext[e + 1, 1, 1 + y, 1 + z] = jnp.where(row4 < 3, tile + time_step * v, tile)
        return carry

    lax.fori_loop(0, 3, evaluate, 0)
    for y, z in cells:
        for k in range(3):
            out_pos[k, y, pl.ds(z, 1)] = ext[2, 1, 1 + y, 1 + z][k : k + 1]
            out_vel[k, y, pl.ds(z, 1)] = vel[2 * y + z][k : k + 1]

    def drain(e, carry):
        for group in range(3):
            wait(ext, e, pos_send, group)
            wait(slo, e, slo_send, group)
        return carry

    lax.fori_loop(0, 3, drain, 0)


def on_device(positions, velocities, species, counts):
    vmem = pl.BlockSpec(memory_space=pltpu.VMEM)
    shape = jax.ShapeDtypeStruct((3, 2, 2, 128), f32)
    new_positions, new_velocities = pl.pallas_call(
        kernel,
        out_shape=(shape, shape),
        in_specs=[vmem, vmem, vmem, pl.BlockSpec(memory_space=pltpu.SMEM)],
        out_specs=(vmem, vmem),
        scratch_shapes=[
            pltpu.VMEM((4, 3, 4, 4, 4, 128), f32),
            pltpu.VMEM((3, 3, 4, 4, 1, 128), f32),
            pltpu.VMEM((12, 32, 512), bf16),
            pltpu.VMEM((12, 8, 512), f32),
            pltpu.VMEM((12, 16, 512), bf16),
            pltpu.VMEM((4, 128, 32), bf16),
            pltpu.VMEM((4, 3, 128, 128), f32),
            pltpu.VMEM((4, 128, 128), f32),
            pltpu.VMEM((4, 128, 16), f32),
            pltpu.VMEM((4, 4, 128), f32),
        ]
        + [pltpu.SemaphoreType.DMA((3, 3))] * 4,
        compiler_params=pltpu.CompilerParams(
            collective_id=0, has_side_effects=True, vmem_limit_bytes=32 * 1024 * 1024
        ),
    )(positions[:, 0], velocities[:, 0], species[0], counts[0])
    return new_positions[:, None], new_velocities[:, None]


def solution(mesh):
    return jax.shard_map(
        on_device,
        mesh=mesh,
        in_specs=(
            P(None, "gx", "gy", "gz", None),
            P(None, "gx", "gy", "gz", None),
            P("gx", "gy", "gz", None),
            P("gx", "gy", "gz"),
        ),
        out_specs=(P(None, "gx", "gy", "gz", None), P(None, "gx", "gy", "gz", None)),
        check_vma=False,
    )
```

```python
import functools
import itertools

import jax
import jax.numpy as jnp
from jax import lax
from jax.experimental import pallas as pl
from jax.experimental.pallas import tpu as pltpu
from jax.sharding import PartitionSpec as P

MESH = pl.DeviceIdType.MESH
time_step = 0.05
AXES = ("gx", "gy", "gz")
SOURCE = {0: (1, 2), 1: (2, 1), -1: (1, 1)}
TARGET = {0: 1, 1: 0, -1: 3}
DIRECTIONS = sorted(
    (d for d in itertools.product((-1, 0, 1), repeat=3) if d != (0, 0, 0)),
    key=lambda d: -(4 * abs(d[0] * d[1]) + 2 * abs(d[0]) + 2 * abs(d[1]) + abs(d[2])),
)
f32, bf16 = jnp.float32, jnp.bfloat16
CHUNKS = (128, 64, 128)


def group_of(d):
    return 0 if d[0] == 0 else (1 if d[1] == 0 else 2)


def group_ref(buffer, group):
    return buffer.at[1, pl.ds(0, 3)] if group == 0 else buffer.at[0]


def group_cell(group, index):
    if group == 0:
        return 1, index
    if group == 1:
        return 2 * (index // 2), 1 + index % 2
    return 2 * (index // 2), 3 * (index % 2)


def pieces(value):
    high = value.astype(bf16).astype(f32)
    rest = value - high
    middle = rest.astype(bf16).astype(f32)
    return high, middle, rest - middle


def strength_of(amplitude):
    return jnp.where(amplitude > 1.15, 0.4, jnp.where(amplitude > 0.0, 0.3, 0.0)).astype(f32)


def kernel(
    pos_ref, vel_ref, spec_ref, count_ref, out_pos, out_vel,
    ext, slo, part, rows, lhs, own, near, acc, total, vel,
    pos_send, pos_recv, slo_send, slo_recv,
):
    place = [lax.axis_index(a) for a in AXES]
    sizes = [lax.axis_size(a) for a in AXES]

    def device(d):
        return tuple(lax.rem(m + k + s, k) for m, k, s in zip(place, sizes, d))

    barrier = pltpu.get_barrier_semaphore()
    for d in DIRECTIONS:
        pl.semaphore_signal(barrier, inc=1, device_id=device(d), device_id_type=MESH)

    row4 = lax.broadcasted_iota(jnp.int32, (4, 128), 0)
    slot = lax.broadcasted_iota(jnp.int32, (1, 128), 1)
    cells = [(y, z) for y in range(2) for z in range(2)]
    for y, z in cells:
        c = 2 * y + z
        present = slot < count_ref[y, z]
        species = spec_ref[y, pl.ds(z, 1)]
        amplitude = jnp.where(present, jnp.where(species == 1, 1.3, 1.0), 0.0).astype(f32)
        inverse_mass = jnp.where(species == 1, 1.6, 1.0).astype(f32)
        ext[0, 1, 1 + y, 1 + z] = jnp.concatenate([pos_ref[k, y, pl.ds(z, 1)] for k in range(3)] + [amplitude], axis=0)
        vel[c] = jnp.concatenate([vel_ref[k, y, pl.ds(z, 1)] for k in range(3)] + [inverse_mass], axis=0)

    pl.semaphore_wait(barrier, len(DIRECTIONS))

    def send(buffer, e, send_sem, recv_sem):
        for d in DIRECTIONS:
            dx, dy, dz = d
            (sy, ny), (sz, nz) = SOURCE[dy], SOURCE[dz]
            pltpu.make_async_remote_copy(
                src_ref=buffer.at[e, 1, pl.ds(sy, ny), pl.ds(sz, nz)],
                dst_ref=buffer.at[e, 1 - dx, pl.ds(TARGET[dy], ny), pl.ds(TARGET[dz], nz)],
                send_sem=send_sem.at[e, group_of(d)],
                recv_sem=recv_sem.at[e, group_of(d)],
                device_id=device(d),
                device_id_type=MESH,
            ).start()

    def wait(buffer, e, sem, group):
        ref = group_ref(buffer.at[e], group)
        pltpu.make_async_copy(ref, ref, sem.at[e, group]).wait()

    def shift_of(ix, iy, iz):
        fx, fy = (jnp.asarray(v, jnp.int32).astype(f32) for v in (ix, iy))
        return jnp.where(row4 == 0, fx - 1.5, jnp.where(row4 == 1, fy - 2.0, float(iz - 2)))

    def keep(line, k, lanes, value):
        rows[line, k, :, lanes] = jnp.broadcast_to(value, (8, 128))

    def prepare(e, group):
        def one(index, carry):
            ix, iy = group_cell(group, index)
            line = 4 * ix + iy
            for iz in range(4):
                lanes = pl.ds(128 * iz, 128)
                tile = ext[e, ix, iy, iz]
                place_ = tile + shift_of(ix, iy, iz)
                square = jnp.sum(jnp.where(row4 < 3, place_ * place_, 0.0), axis=0, keepdims=True)
                h, m, l = pieces(jnp.where(row4 < 3, place_, square))
                one_ = jnp.ones_like(h)
                zero = jnp.zeros_like(h)
                part[line, :, lanes] = jnp.concatenate([h, m, h, m, l, h, one_, zero], axis=0).astype(bf16)
                amplitude = tile[3:4]
                keep(line, 0, lanes, amplitude)
                keep(line, 1, lanes, 2.0 * strength_of(amplitude))
                for k in range(3):
                    keep(line, 2 + k, lanes, place_[k : k + 1])
            return carry

        lax.fori_loop(0, 4, one, 0)

    def lines_of(group, y):
        if group == 0:
            return [4 + y + k for k in range(3)]
        if group == 1:
            return [1, 2, 9, 10]
        return [3 * y, 8 + 3 * y]

    def smooth(group):
        def one(c, line, z):
            t = jnp.dot(lhs[c], part[line, :, pl.ds(128 * z, 384)], preferred_element_type=f32)
            near[c, line] = jnp.maximum(t, 0.0)

        if group == 2:
            for y, z in cells:
                for line in lines_of(2, y):
                    one(2 * y + z, line, z)
        else:

            def step(k, carry):
                for y, z in cells:
                    one(2 * y + z, 4 + y + k if group == 0 else 8 * (k // 2) + 1 + k % 2, z)
                return carry

            lax.fori_loop(0, 3 + group, step, 0)

    def sweep(count, body):
        def one(index, carry):
            parts = 128 // count
            c = index // parts
            body(c, c // 2, c % 2, pl.ds(pl.multiple_of(count * (index % parts), count), count))
            return carry

        lax.fori_loop(0, 4 * (128 // count), one, 0)

    def tiles(lines, z):
        for line in lines:
            for k in range(3):
                yield line, pl.ds(128 * k, 128), pl.ds(pl.multiple_of(128 * (z + k), 128), 128)

    def fold(value):
        return value.reshape(-1, 8, 128)

    def add_density(group):
        def body(c, y, z, chunk):
            level = fold(acc[c, 0, chunk])
            for line, at, lanes in tiles(lines_of(group, y), z):
                s = fold(near[c, line, chunk, at])
                level = level + s * s * (s * rows[line, 0, :, lanes])
            acc[c, 0, chunk] = level.reshape(-1, 128)

        sweep(CHUNKS[0], body)

    def first_forces():
        def body(c, y, z, chunk):
            slope, strength = fold(own[c, 0, chunk]), fold(own[c, 1, chunk])
            sums = [jnp.zeros(slope.shape, f32) for _ in range(4)]
            for line, at, lanes in tiles([4 * ix + y + k for ix in range(3) for k in range(3)], z):
                s = fold(near[c, line, chunk, at])
                square = s * s
                near[c, line, chunk, at] = square.reshape(-1, 128)
                w = square * (slope * rows[line, 0, :, lanes]) + s * (strength * rows[line, 1, :, lanes])
                sums[3] = sums[3] + w
                for k in range(3):
                    sums[k] = sums[k] + w * rows[line, 2 + k, :, lanes]
            for k in range(4):
                acc[c, k, chunk] = sums[k].reshape(-1, 128)

        sweep(CHUNKS[1], body)

    def add_forces(group):
        def body(c, y, z, chunk):
            sums = [fold(acc[c, k, chunk]) for k in range(4)]
            for line, at, lanes in tiles(lines_of(group, y), z):
                square = fold(near[c, line, chunk, at])
                for k in range(4):
                    sums[k] = sums[k] + square * rows[line, 5 + k, :, lanes]
            for k in range(4):
                acc[c, k, chunk] = sums[k].reshape(-1, 128)

        sweep(CHUNKS[2], body)

    def lane_sums(c):
        return jnp.concatenate([jnp.sum(jnp.transpose(acc[c, k]), axis=0, keepdims=True) for k in range(4)], axis=0)

    def across_rows(value):
        return jnp.transpose(jnp.broadcast_to(value, (128, 128)))

    def evaluate(e, carry):
        send(ext, e, pos_send, pos_recv)
        for y, z in cells:
            c = 2 * y + z
            place_ = ext[e, 1, 1 + y, 1 + z] + shift_of(1, 1 + y, 1 + z)
            square = jnp.sum(jnp.where(row4 < 3, place_ * place_, 0.0), axis=0, keepdims=True)
            h, m, l = pieces(2.0 * place_)
            th, tm, tl = pieces(1.0 - square)
            last = lambda v, fill: jnp.where(row4 < 3, v, fill)
            ends = jnp.where(row4 == 0, th, jnp.where(row4 == 1, tm, jnp.where(row4 == 2, tl, 0.0)))
            side = jnp.concatenate(
                [last(h, -1.0), last(h, -1.0), last(m, 0.0), last(m, 0.0), last(h, -1.0), last(l, 0.0), ends, jnp.zeros_like(h)],
                axis=0,
            )
            lhs[c] = jnp.transpose(side).astype(bf16)
            acc[c, 0] = jnp.zeros((128, 128), f32)
            own[c, 1] = across_rows(strength_of(ext[e, 1, 1 + y, 1 + z][3:4]))
        for group in range(3):
            wait(ext, e, pos_recv, group)
            prepare(e, group)
            smooth(group)
            add_density(group)
        for y, z in cells:
            c = 2 * y + z
            amplitude = ext[e, 1, 1 + y, 1 + z][3:4]
            level = jnp.sum(jnp.transpose(acc[c, 0]), axis=0, keepdims=True) - amplitude + 1.0
            slo[e, 1, 1 + y, 1 + z] = jnp.where(amplitude > 0.0, -0.5, 0.0) / jnp.sqrt(level)
        send(slo, e, slo_send, slo_recv)
        for y, z in cells:
            own[2 * y + z, 0] = across_rows(3.0 * slo[e, 1, 1 + y, 1 + z])
        first_forces()
        for c in range(4):
            total[c] = lane_sums(c)
            for k in range(4):
                acc[c, k] = jnp.zeros((128, 128), f32)
        for group in range(3):
            wait(slo, e, slo_recv, group)

            def spread(index, carry):
                ix, iy = group_cell(group, index)
                for iz in range(4):
                    line, lanes = 4 * ix + iy, pl.ds(128 * iz, 128)
                    slope = 3.0 * slo[e, ix, iy, iz]
                    keep(line, 8, lanes, slope)
                    for k in range(3):
                        rows[line, 5 + k, :, lanes] = slope * rows[line, 2 + k, :, lanes]
                return carry

            lax.fori_loop(0, 4, spread, 0)
            add_forces(group)
        kick = jnp.where(e == 1, 2.0, 1.0) * (0.5 * time_step)
        for y, z in cells:
            c = 2 * y + z
            tile = ext[e, 1, 1 + y, 1 + z]
            place_ = tile + shift_of(1, 1 + y, 1 + z)
            r = total[c] + tile[3:4] * lane_sums(c)
            force = -2.0 * (r - place_ * r[3:4])
            v = vel[c]
            v = jnp.where(row4 < 3, v + kick * v[3:4] * force, v)
            vel[c] = v
            ext[e + 1, 1, 1 + y, 1 + z] = jnp.where(row4 < 3, tile + time_step * v, tile)
        return carry

    lax.fori_loop(0, 3, evaluate, 0)
    for y, z in cells:
        for k in range(3):
            out_pos[k, y, pl.ds(z, 1)] = ext[2, 1, 1 + y, 1 + z][k : k + 1]
            out_vel[k, y, pl.ds(z, 1)] = vel[2 * y + z][k : k + 1]

    def drain(e, carry):
        for group in range(3):
            wait(ext, e, pos_send, group)
            wait(slo, e, slo_send, group)
        return carry

    lax.fori_loop(0, 3, drain, 0)


def on_device(positions, velocities, species, counts):
    vmem = pl.BlockSpec(memory_space=pltpu.VMEM)
    shape = jax.ShapeDtypeStruct((3, 2, 2, 128), f32)
    new_positions, new_velocities = pl.pallas_call(
        kernel,
        out_shape=(shape, shape),
        in_specs=[vmem, vmem, vmem, pl.BlockSpec(memory_space=pltpu.SMEM)],
        out_specs=(vmem, vmem),
        scratch_shapes=[
            pltpu.VMEM((4, 3, 4, 4, 4, 128), f32),
            pltpu.VMEM((3, 3, 4, 4, 1, 128), f32),
            pltpu.VMEM((12, 32, 512), bf16),
            pltpu.VMEM((12, 9, 8, 512), f32),
            pltpu.VMEM((4, 128, 32), bf16),
            pltpu.VMEM((4, 2, 128, 128), f32),
            pltpu.VMEM((4, 12, 128, 384), f32),
            pltpu.VMEM((4, 4, 128, 128), f32),
            pltpu.VMEM((4, 4, 128), f32),
            pltpu.VMEM((4, 4, 128), f32),
        ]
        + [pltpu.SemaphoreType.DMA((3, 3))] * 4,
        compiler_params=pltpu.CompilerParams(
            collective_id=0, has_side_effects=True, vmem_limit_bytes=32 * 1024 * 1024
        ),
    )(positions[:, 0], velocities[:, 0], species[0], counts[0])
    return new_positions[:, None], new_velocities[:, None]


def solution(mesh):
    return jax.shard_map(
        on_device,
        mesh=mesh,
        in_specs=(
            P(None, "gx", "gy", "gz", None),
            P(None, "gx", "gy", "gz", None),
            P("gx", "gy", "gz", None),
            P("gx", "gy", "gz"),
        ),
        out_specs=(P(None, "gx", "gy", "gz", None), P(None, "gx", "gy", "gz", None)),
        check_vma=False,
    )
```

```python
import functools
import itertools

import jax
import jax.numpy as jnp
from jax import lax
from jax.experimental import pallas as pl
from jax.experimental.pallas import tpu as pltpu
from jax.sharding import PartitionSpec as P

MESH = pl.DeviceIdType.MESH
time_step = 0.05
AXES = ("gx", "gy", "gz")
SOURCE = {0: (1, 2), 1: (2, 1), -1: (1, 1)}
TARGET = {0: 1, 1: 0, -1: 3}
DIRECTIONS = sorted(
    (d for d in itertools.product((-1, 0, 1), repeat=3) if d != (0, 0, 0)),
    key=lambda d: -(4 * abs(d[0] * d[1]) + 2 * abs(d[0]) + 2 * abs(d[1]) + abs(d[2])),
)
f32, bf16 = jnp.float32, jnp.bfloat16
CHUNK = 64


def group_of(d):
    if d[0] == 0:
        return 0 if d[1] == 0 else 1
    return {0: 2, 1: 3, -1: 4}[d[1]]


def group_ref(buffer, group):
    if isinstance(group, int) and group < 3:
        return (buffer.at[1, 0], buffer.at[1, pl.ds(0, 2)], buffer.at[0])[group]
    return buffer.at[1, pl.ds(0, 2)]


def pieces(value):
    high = value.astype(bf16).astype(f32)
    rest = value - high
    middle = rest.astype(bf16).astype(f32)
    return high, middle, rest - middle


def strength_of(amplitude):
    return jnp.where(amplitude > 1.15, 0.4, jnp.where(amplitude > 0.0, 0.3, 0.0)).astype(f32)


def kernel(
    pos_hbm, vel_hbm, spec_hbm, count_hbm, out_pos, out_vel,
    ext, slo, part, rows, lhs, own, near, acc, total, vel,
    pos_ref, vel_ref, spec_ref, count_ref, pos_send, pos_recv, slo_send, slo_recv, load_sem,
):
    place = [lax.axis_index(a) for a in AXES]
    sizes = [lax.axis_size(a) for a in AXES]

    def device(d):
        return tuple(lax.rem(m + k + s, k) for m, k, s in zip(place, sizes, d))

    barrier = pltpu.get_barrier_semaphore()
    for d in DIRECTIONS:
        pl.semaphore_signal(barrier, inc=1, device_id=device(d), device_id_type=MESH)

    loads = [
        pltpu.make_async_copy(source, target, load_sem.at[k])
        for k, (source, target) in enumerate(
            [(pos_hbm, pos_ref), (spec_hbm, spec_ref), (count_hbm, count_ref), (vel_hbm, vel_ref)]
        )
    ]
    for load in loads:
        load.start()
    for load in loads:
        load.wait()

    row4 = lax.broadcasted_iota(jnp.int32, (4, 128), 0)
    slot = lax.broadcasted_iota(jnp.int32, (1, 128), 1)
    cells = [(y, z) for y in range(2) for z in range(2)]
    for y, z in cells:
        c = 2 * y + z
        present = slot < count_ref[pl.ds(y, 1), pl.ds(z, 1)]
        species = spec_ref[y, pl.ds(z, 1)]
        amplitude = jnp.where(present, jnp.where(species == 1, 1.3, 1.0), 0.0).astype(f32)
        inverse_mass = jnp.where(species == 1, 1.6, 1.0).astype(f32)
        ext[0, 1, 1 + y, 1 + z] = jnp.concatenate([pos_ref[k, y, pl.ds(z, 1)] for k in range(3)] + [amplitude], axis=0)
        vel[c] = jnp.concatenate([vel_ref[k, y, pl.ds(z, 1)] for k in range(3)] + [inverse_mass], axis=0)

    pl.semaphore_wait(barrier, len(DIRECTIONS))

    def send(buffer, e, send_sem, recv_sem):
        for d in DIRECTIONS:
            dx, dy, dz = d
            (sy, ny), (sz, nz) = SOURCE[dy], SOURCE[dz]
            pltpu.make_async_remote_copy(
                src_ref=buffer.at[e, 1, pl.ds(sy, ny), pl.ds(sz, nz)],
                dst_ref=buffer.at[e, 1 - dx, pl.ds(TARGET[dy], ny), pl.ds(TARGET[dz], nz)],
                send_sem=send_sem.at[e, group_of(d)],
                recv_sem=recv_sem.at[e, group_of(d)],
                device_id=device(d),
                device_id_type=MESH,
            ).start()

    def wait(buffer, e, sem, group):
        ref = group_ref(buffer.at[e], group)
        pltpu.make_async_copy(ref, ref, sem.at[e, group]).wait()

    def shift_of(ix, iy, iz):
        fx, fy = (jnp.asarray(v, jnp.int32).astype(f32) for v in (ix, iy))
        return jnp.where(row4 == 0, fx - 1.5, jnp.where(row4 == 1, fy - 2.0, float(iz - 2)))

    def keep(line, k, lanes, value):
        rows[line, k, :, lanes] = jnp.broadcast_to(value, (8, 128))

    def prepare(e, count, line_at):
        def one(index, carry):
            line = line_at(index)
            ix, iy = line // 4, line % 4
            for iz in range(4):
                lanes = pl.ds(128 * iz, 128)
                tile = ext[e, ix, iy, iz]
                place_ = tile + shift_of(ix, iy, iz)
                square = jnp.sum(jnp.where(row4 < 3, place_ * place_, 0.0), axis=0, keepdims=True)
                h, m, l = pieces(jnp.where(row4 < 3, place_, square))
                one_ = jnp.ones_like(h)
                zero = jnp.zeros_like(h)
                part[line, :, lanes] = jnp.concatenate([h, m, h, m, l, h, one_, zero], axis=0).astype(bf16)
                amplitude = tile[3:4]
                keep(line, 0, lanes, amplitude)
                keep(line, 1, lanes, 2.0 * strength_of(amplitude))
                for k in range(3):
                    keep(line, 2 + k, lanes, place_[k : k + 1])
            return carry

        lax.fori_loop(0, count, one, 0)

    last = lax.rem(place[0] + 1, 2)
    side_of = {3: 1 - last, 4: last}

    fetched = {
        0: (2, lambda k: 5 + k),
        1: (2, lambda k: 4 + 3 * k),
        2: (4, lambda k: 8 * (k // 2) + 1 + k % 2),
        3: (2, lambda k: 8 * k + 3 * side_of[3]),
        4: (2, lambda k: 8 * k + 3 * side_of[4]),
    }

    def met(group):
        if group == 0:
            return [(y, [5, 6]) for y in range(2)]
        if group == 1:
            return [(y, [4 + 3 * y]) for y in range(2)]
        if group == 2:
            return [(y, [1, 2, 9, 10]) for y in range(2)]
        y = side_of[group]
        return [(y, [3 * y, 8 + 3 * y])]

    def strip(c, line, z):
        t = jnp.dot(lhs[c], part[line, :, pl.ds(128 * z, 384)], preferred_element_type=f32)
        s = jnp.maximum(t, 0.0)
        near[c, line] = s
        return s

    def weighted(s, line, z):
        out = None
        for k in range(3):
            v = fold(s[:, 128 * k : 128 * k + 128])
            v = v * v * (v * rows[line, 0, :, pl.ds(128 * (z + k), 128)])
            out = v if out is None else out + v
        return out.reshape(128, 128)

    def densities(group):
        if group == 2:

            def step(k, carry):
                line = 8 * (k // 2) + 1 + k % 2
                for y, z in cells:
                    c = 2 * y + z
                    acc[c, 0] += weighted(strip(c, line, z), line, z)
                return carry

            lax.fori_loop(0, 4, step, 0)
        else:
            for y, lines in met(group):
                for z in range(2):
                    c = 2 * y + z
                    acc[c, 0] += sum(weighted(strip(c, line, z), line, z) for line in lines)

    def sweep(count, body):
        def one(index, carry):
            parts = 128 // count
            c = index // parts
            body(c, c // 2, c % 2, pl.ds(pl.multiple_of(count * (index % parts), count), count))
            return carry

        lax.fori_loop(0, 4 * (128 // count), one, 0)

    def tiles(lines, z):
        for line in lines:
            for k in range(3):
                yield line, pl.ds(128 * k, 128), pl.ds(pl.multiple_of(128 * (z + k), 128), 128)

    def fold(value):
        return value.reshape(-1, 8, 128)

    def first_forces():
        def body(c, y, z, chunk):
            slope, strength = fold(own[c, 0, chunk]), fold(own[c, 1, chunk])
            sums = [jnp.zeros(slope.shape, f32) for _ in range(4)]
            for line, at, lanes in tiles([4 * ix + y + k for ix in range(3) for k in range(3)], z):
                s = fold(near[c, line, chunk, at])
                square = s * s
                near[c, line, chunk, at] = square.reshape(-1, 128)
                w = square * (slope * rows[line, 0, :, lanes]) + s * (strength * rows[line, 1, :, lanes])
                sums[3] = sums[3] + w
                for k in range(3):
                    sums[k] = sums[k] + w * rows[line, 2 + k, :, lanes]
            for k in range(4):
                acc[c, k, chunk] = sums[k].reshape(-1, 128)

        sweep(CHUNK, body)

    def add_forces(group):
        def body(c, lines, z):
            sums = [fold(acc[c, k]) for k in range(4)]
            for line, at, lanes in tiles(lines, z):
                square = fold(near[c, line, :, at])
                for k in range(4):
                    sums[k] = sums[k] + square * rows[line, 5 + k, :, lanes]
            for k in range(4):
                acc[c, k] = sums[k].reshape(128, 128)

        def one(c, carry):
            y, z = c // 2, c % 2
            body(c, {0: [5, 6], 1: [4 + 3 * y], 2: [1, 2, 9, 10]}[group], z)
            return carry

        if group < 3:
            lax.fori_loop(0, 4, one, 0)
        else:
            y = side_of[group]
            for z in range(2):
                body(2 * y + z, [3 * y, 8 + 3 * y], z)

    def lane_sums(c):
        return jnp.concatenate([jnp.sum(jnp.transpose(acc[c, k]), axis=0, keepdims=True) for k in range(4)], axis=0)

    def across_rows(value):
        return jnp.transpose(jnp.broadcast_to(value, (128, 128)))

    def arrival(group):
        return group if group < 3 else 3 + side_of[group]

    def evaluate(e, carry):
        send(ext, e, pos_send, pos_recv)
        for y, z in cells:
            c = 2 * y + z
            place_ = ext[e, 1, 1 + y, 1 + z] + shift_of(1, 1 + y, 1 + z)
            square = jnp.sum(jnp.where(row4 < 3, place_ * place_, 0.0), axis=0, keepdims=True)
            h, m, l = pieces(2.0 * place_)
            th, tm, tl = pieces(1.0 - square)
            end = lambda v, fill: jnp.where(row4 < 3, v, fill)
            ends = jnp.where(row4 == 0, th, jnp.where(row4 == 1, tm, jnp.where(row4 == 2, tl, 0.0)))
            side = jnp.concatenate(
                [end(h, -1.0), end(h, -1.0), end(m, 0.0), end(m, 0.0), end(h, -1.0), end(l, 0.0), ends, jnp.zeros_like(h)],
                axis=0,
            )
            lhs[c] = jnp.transpose(side).astype(bf16)
            acc[c, 0] = jnp.zeros((128, 128), f32)
            own[c, 1] = across_rows(strength_of(ext[e, 1, 1 + y, 1 + z][3:4]))
        for group in range(5):
            wait(ext, e, pos_recv, arrival(group))
            prepare(e, *fetched[group])
            densities(group)
        for y, z in cells:
            c = 2 * y + z
            amplitude = ext[e, 1, 1 + y, 1 + z][3:4]
            level = jnp.sum(jnp.transpose(acc[c, 0]), axis=0, keepdims=True) - amplitude + 1.0
            slo[e, 1, 1 + y, 1 + z] = jnp.where(amplitude > 0.0, -0.5, 0.0) / jnp.sqrt(level)
        send(slo, e, slo_send, slo_recv)
        for y, z in cells:
            own[2 * y + z, 0] = across_rows(3.0 * slo[e, 1, 1 + y, 1 + z])
        first_forces()
        for c in range(4):
            total[c] = lane_sums(c)
            for k in range(4):
                acc[c, k] = jnp.zeros((128, 128), f32)
        for group in range(5):
            wait(slo, e, slo_recv, arrival(group))
            count, line_at = fetched[group]

            def spread(index, carry):
                line = line_at(index)
                ix, iy = line // 4, line % 4
                for iz in range(4):
                    lanes = pl.ds(128 * iz, 128)
                    slope = 3.0 * slo[e, ix, iy, iz]
                    keep(line, 8, lanes, slope)
                    for k in range(3):
                        rows[line, 5 + k, :, lanes] = slope * rows[line, 2 + k, :, lanes]
                return carry

            lax.fori_loop(0, count, spread, 0)
            add_forces(group)
        kick = jnp.where(e == 1, 2.0, 1.0) * (0.5 * time_step)
        for y, z in cells:
            c = 2 * y + z
            tile = ext[e, 1, 1 + y, 1 + z]
            place_ = tile + shift_of(1, 1 + y, 1 + z)
            r = total[c] + tile[3:4] * lane_sums(c)
            force = -2.0 * (r - place_ * r[3:4])
            v = vel[c]
            v = jnp.where(row4 < 3, v + kick * v[3:4] * force, v)
            vel[c] = v
            ext[e + 1, 1, 1 + y, 1 + z] = jnp.where(row4 < 3, tile + time_step * v, tile)
        return carry

    lax.fori_loop(0, 3, evaluate, 0)
    for y, z in cells:
        for k in range(3):
            out_pos[k, y, pl.ds(z, 1)] = ext[2, 1, 1 + y, 1 + z][k : k + 1]
            out_vel[k, y, pl.ds(z, 1)] = vel[2 * y + z][k : k + 1]

    def drain(e, carry):
        for group in range(5):
            wait(ext, e, pos_send, group)
            wait(slo, e, slo_send, group)
        return carry

    lax.fori_loop(0, 3, drain, 0)


def on_device(positions, velocities, species, counts):
    vmem = pl.BlockSpec(memory_space=pltpu.VMEM)
    shape = jax.ShapeDtypeStruct((3, 2, 2, 128), f32)
    new_positions, new_velocities = pl.pallas_call(
        kernel,
        out_shape=(shape, shape),
        in_specs=[pl.BlockSpec(memory_space=pltpu.HBM)] * 4,
        out_specs=(vmem, vmem),
        scratch_shapes=[
            pltpu.VMEM((4, 3, 4, 4, 4, 128), f32),
            pltpu.VMEM((3, 3, 4, 4, 1, 128), f32),
            pltpu.VMEM((12, 32, 512), bf16),
            pltpu.VMEM((12, 9, 8, 512), f32),
            pltpu.VMEM((4, 128, 32), bf16),
            pltpu.VMEM((4, 2, 128, 128), f32),
            pltpu.VMEM((4, 12, 128, 384), f32),
            pltpu.VMEM((4, 4, 128, 128), f32),
            pltpu.VMEM((4, 4, 128), f32),
            pltpu.VMEM((4, 4, 128), f32),
        ]
        + [pltpu.VMEM((3, 2, 2, 128), f32)] * 2
        + [pltpu.VMEM((2, 2, 128), jnp.int32), pltpu.VMEM((2, 2), jnp.int32)]
        + [pltpu.SemaphoreType.DMA((3, 5))] * 4
        + [pltpu.SemaphoreType.DMA((4,))],
        compiler_params=pltpu.CompilerParams(
            collective_id=0, has_side_effects=True, vmem_limit_bytes=32 * 1024 * 1024
        ),
    )(*(pltpu.with_memory_space_constraint(a, pltpu.HBM) for a in (positions[:, 0], velocities[:, 0], species[0], counts[0])))
    return new_positions[:, None], new_velocities[:, None]


def solution(mesh):
    return jax.shard_map(
        on_device,
        mesh=mesh,
        in_specs=(
            P(None, "gx", "gy", "gz", None),
            P(None, "gx", "gy", "gz", None),
            P("gx", "gy", "gz", None),
            P("gx", "gy", "gz"),
        ),
        out_specs=(P(None, "gx", "gy", "gz", None), P(None, "gx", "gy", "gz", None)),
        check_vma=False,
    )
```

```python
import functools
import itertools

import jax
import jax.numpy as jnp
from jax import lax
from jax.experimental import pallas as pl
from jax.experimental.pallas import tpu as pltpu
from jax.sharding import PartitionSpec as P

MESH = pl.DeviceIdType.MESH
time_step = 0.05
AXES = ("gx", "gy", "gz")
SOURCE = {0: (1, 2), 1: (2, 1), -1: (1, 1)}
TARGET = {0: 1, 1: 0, -1: 3}
DIRECTIONS = sorted(
    (d for d in itertools.product((-1, 0, 1), repeat=3) if d != (0, 0, 0)),
    key=lambda d: -(4 * abs(d[0] * d[1]) + 2 * abs(d[0]) + 2 * abs(d[1]) + abs(d[2])),
)
f32, bf16 = jnp.float32, jnp.bfloat16
CHUNK = 64


def group_of(d):
    if d[0] == 0:
        return 0 if d[1] == 0 else 1
    if d[1] == 0:
        return 2 if d[2] == 0 else 3
    return 4 if d[1] == 1 else 5


def group_ref(buffer, group):
    if isinstance(group, int) and group == 0:
        return buffer.at[1, 0]
    return buffer.at[1, pl.ds(0, 2)]


def pieces(value):
    high = value.astype(bf16).astype(f32)
    rest = value - high
    middle = rest.astype(bf16).astype(f32)
    return high, middle, rest - middle


def strength_of(amplitude):
    return jnp.where(amplitude > 1.15, 0.4, jnp.where(amplitude > 0.0, 0.3, 0.0)).astype(f32)


def kernel(
    pos_hbm, vel_hbm, spec_hbm, count_hbm, out_pos, out_vel, out_push,
    ext, slo, part, rows, lhs, own, near, acc, total, vel,
    pos_ref, vel_ref, spec_ref, count_ref, pos_send, pos_recv, slo_send, slo_recv, load_sem,
):
    place = [lax.axis_index(a) for a in AXES]
    sizes = [lax.axis_size(a) for a in AXES]

    def device(d):
        return tuple(lax.rem(m + k + s, k) for m, k, s in zip(place, sizes, d))

    barrier = pltpu.get_barrier_semaphore()
    for d in DIRECTIONS:
        pl.semaphore_signal(barrier, inc=1, device_id=device(d), device_id_type=MESH)

    loads = [
        pltpu.make_async_copy(source, target, load_sem.at[k])
        for k, (source, target) in enumerate(
            [(pos_hbm, pos_ref), (spec_hbm, spec_ref), (count_hbm, count_ref), (vel_hbm, vel_ref)]
        )
    ]
    for load in loads:
        load.start()
    for load in loads:
        load.wait()

    row4 = lax.broadcasted_iota(jnp.int32, (4, 128), 0)
    slot = lax.broadcasted_iota(jnp.int32, (1, 128), 1)
    cells = [(y, z) for y in range(2) for z in range(2)]
    for y, z in cells:
        c = 2 * y + z
        present = slot < count_ref[pl.ds(y, 1), pl.ds(z, 1)]
        species = spec_ref[y, pl.ds(z, 1)]
        amplitude = jnp.where(present, jnp.where(species == 1, 1.3, 1.0), 0.0).astype(f32)
        inverse_mass = jnp.where(species == 1, 1.6, 1.0).astype(f32)
        ext[0, 1, 1 + y, 1 + z] = jnp.concatenate([pos_ref[k, y, pl.ds(z, 1)] for k in range(3)] + [amplitude], axis=0)
        vel[c] = jnp.concatenate([vel_ref[k, y, pl.ds(z, 1)] for k in range(3)] + [inverse_mass], axis=0)

    pl.semaphore_wait(barrier, len(DIRECTIONS))

    def send(buffer, e, send_sem, recv_sem):
        for d in DIRECTIONS:
            dx, dy, dz = d
            (sy, ny), (sz, nz) = SOURCE[dy], SOURCE[dz]
            pltpu.make_async_remote_copy(
                src_ref=buffer.at[e, 1, pl.ds(sy, ny), pl.ds(sz, nz)],
                dst_ref=buffer.at[e, 1 - dx, pl.ds(TARGET[dy], ny), pl.ds(TARGET[dz], nz)],
                send_sem=send_sem.at[e, group_of(d)],
                recv_sem=recv_sem.at[e, group_of(d)],
                device_id=device(d),
                device_id_type=MESH,
            ).start()

    def wait(buffer, e, sem, group):
        ref = group_ref(buffer.at[e], group)
        pltpu.make_async_copy(ref, ref, sem.at[e, group]).wait()

    def shift_of(ix, iy, iz):
        fx, fy = (jnp.asarray(v, jnp.int32).astype(f32) for v in (ix, iy))
        return jnp.where(row4 == 0, fx - 1.5, jnp.where(row4 == 1, fy - 2.0, float(iz - 2)))

    def keep(line, k, lanes, value):
        rows[line, k, :, lanes] = jnp.broadcast_to(value, (8, 128))

    def prepare(e, columns, count, line_at):
        def one(index, carry):
            line = line_at(index)
            ix, iy = line // 4, line % 4
            for iz in columns:
                lanes = pl.ds(128 * iz, 128)
                tile = ext[e, ix, iy, iz]
                place_ = tile + shift_of(ix, iy, iz)
                square = jnp.sum(jnp.where(row4 < 3, place_ * place_, 0.0), axis=0, keepdims=True)
                h, m, l = pieces(jnp.where(row4 < 3, place_, square))
                one_ = jnp.ones_like(h)
                zero = jnp.zeros_like(h)
                part[line, :, lanes] = jnp.concatenate([h, m, h, m, l, h, one_, zero], axis=0).astype(bf16)
                amplitude = tile[3:4]
                keep(line, 0, lanes, amplitude)
                keep(line, 1, lanes, 2.0 * strength_of(amplitude))
                for k in range(3):
                    keep(line, 2 + k, lanes, place_[k : k + 1])
            return carry

        lax.fori_loop(0, count, one, 0)

    last = lax.rem(place[0] + 1, 2)
    side_of = {4: 1 - last, 5: last}

    fetched = {
        0: (2, lambda k: 5 + k),
        1: (2, lambda k: 4 + 3 * k),
        2: (4, lambda k: 8 * (k // 2) + 1 + k % 2),
        4: (2, lambda k: 8 * k + 3 * side_of[4]),
        5: (2, lambda k: 8 * k + 3 * side_of[5]),
    }

    def weighted(s, line, z):
        out = None
        for k in range(s.shape[1] // 128):
            v = fold(s[:, 128 * k : 128 * k + 128])
            v = v * v * (v * rows[line, 0, :, pl.ds(128 * (z + k), 128)])
            out = v if out is None else out + v
        return out.reshape(128, 128)

    def smooth(first, count, line, lanes):
        t = jnp.dot(lhs[pl.ds(first, count)], part[line, :, lanes], preferred_element_type=f32)
        return jnp.maximum(t, 0.0)

    def strips(y, lines):
        for z in range(2):
            total_ = 0.0
            for line in lines:
                s = smooth(pl.multiple_of(256 * z + 128 * y, 128), 128, line, pl.ds(128 * z, 384))
                near[2 * y + z, line] = s
                total_ = total_ + weighted(s, line, z)
            acc[2 * y + z, 0] += total_

    def core(line):
        s = smooth(0, 512, line, pl.ds(128, 256))
        for y, z in cells:
            mine = s[256 * z + 128 * y : 256 * z + 128 * y + 128]
            near[2 * y + z, line, :, pl.ds(128 - 128 * z, 256)] = mine
            acc[2 * y + z, 0] += weighted(mine, line, 1)

    def rim(lines):
        for z in range(2):
            found = [smooth(256 * z, 256, line, pl.ds(384 * z, 128)) for line in lines]
            for y in range(2):
                extra = 0.0
                for line, s in zip(lines, found):
                    mine = s[128 * y : 128 * y + 128]
                    near[2 * y + z, line, :, pl.ds(256 * z, 128)] = mine
                    extra = extra + weighted(mine, line, 3 * z)
                acc[2 * y + z, 0] += extra

    def sweep(count, body):
        def one(index, carry):
            parts = 128 // count
            c = index // parts
            body(c, c // 2, c % 2, pl.ds(pl.multiple_of(count * (index % parts), count), count))
            return carry

        lax.fori_loop(0, 4 * (128 // count), one, 0)

    def tiles(lines, z):
        for line in lines:
            for k in range(3):
                yield line, pl.ds(128 * k, 128), pl.ds(pl.multiple_of(128 * (z + k), 128), 128)

    def fold(value):
        return value.reshape(-1, 8, 128)

    def first_forces():
        def body(c, y, z, chunk):
            slope, strength = fold(own[c, 0, chunk]), fold(own[c, 1, chunk])
            sums = [jnp.zeros(slope.shape, f32) for _ in range(4)]
            for line, at, lanes in tiles([4 * ix + y + k for ix in range(3) for k in range(3)], z):
                s = fold(near[c, line, chunk, at])
                square = s * s
                near[c, line, chunk, at] = square.reshape(-1, 128)
                w = square * (slope * rows[line, 0, :, lanes]) + s * (strength * rows[line, 1, :, lanes])
                sums[3] = sums[3] + w
                for k in range(3):
                    sums[k] = sums[k] + w * rows[line, 2 + k, :, lanes]
            for k in range(4):
                acc[c, k, chunk] = sums[k].reshape(-1, 128)

        sweep(CHUNK, body)

    def add_forces(group):
        def body(c, lines, z):
            sums = [fold(acc[c, k]) for k in range(4)]
            for line, at, lanes in tiles(lines, z):
                square = fold(near[c, line, :, at])
                for k in range(4):
                    sums[k] = sums[k] + square * rows[line, 5 + k, :, lanes]
            for k in range(4):
                acc[c, k] = sums[k].reshape(128, 128)

        def one(c, carry):
            y, z = c // 2, c % 2
            body(c, {0: [5, 6], 1: [4 + 3 * y], 2: [1, 2, 9, 10]}[group], z)
            return carry

        if group < 4:
            lax.fori_loop(0, 4, one, 0)
        else:
            y = side_of[group]
            for z in range(2):
                body(2 * y + z, [3 * y, 8 + 3 * y], z)

    def lane_sums(c):
        return jnp.concatenate([jnp.sum(jnp.transpose(acc[c, k]), axis=0, keepdims=True) for k in range(4)], axis=0)

    def across_rows(value):
        return jnp.transpose(jnp.broadcast_to(value, (128, 128)))

    def arrival(group):
        return group if group < 4 else 4 + side_of[group]

    def evaluate(e, carry):
        send(ext, e, pos_send, pos_recv)
        for y, z in cells:
            c = 2 * y + z
            place_ = ext[e, 1, 1 + y, 1 + z] + shift_of(1, 1 + y, 1 + z)
            square = jnp.sum(jnp.where(row4 < 3, place_ * place_, 0.0), axis=0, keepdims=True)
            h, m, l = pieces(2.0 * place_)
            th, tm, tl = pieces(1.0 - square)
            end = lambda v, fill: jnp.where(row4 < 3, v, fill)
            ends = jnp.where(row4 == 0, th, jnp.where(row4 == 1, tm, jnp.where(row4 == 2, tl, 0.0)))
            side = jnp.concatenate(
                [end(h, -1.0), end(h, -1.0), end(m, 0.0), end(m, 0.0), end(h, -1.0), end(l, 0.0), ends, jnp.zeros_like(h)],
                axis=0,
            )
            lhs[pl.ds(256 * z + 128 * y, 128)] = jnp.transpose(side).astype(bf16)
            acc[c, 0] = jnp.zeros((128, 128), f32)
            own[c, 1] = across_rows(strength_of(ext[e, 1, 1 + y, 1 + z][3:4]))
        prepare(e, (1, 2), *fetched[0])
        core(5)
        core(6)
        wait(ext, e, pos_recv, 0)
        prepare(e, (0, 3), *fetched[0])
        rim([5, 6])
        wait(ext, e, pos_recv, 2)
        prepare(e, (1, 2), *fetched[2])
        for line in (1, 2, 9, 10):
            core(line)
        wait(ext, e, pos_recv, 3)
        prepare(e, (0, 3), *fetched[2])
        rim([1, 2, 9, 10])
        wait(ext, e, pos_recv, 1)
        prepare(e, range(4), *fetched[1])
        for y in range(2):
            strips(y, [4 + 3 * y])
        for group in (4, 5):
            wait(ext, e, pos_recv, arrival(group))
            prepare(e, range(4), *fetched[group])
            y = side_of[group]
            strips(y, [3 * y, 8 + 3 * y])
        for y, z in cells:
            c = 2 * y + z
            amplitude = ext[e, 1, 1 + y, 1 + z][3:4]
            level = jnp.sum(jnp.transpose(acc[c, 0]), axis=0, keepdims=True) - amplitude + 1.0
            slo[e, 1, 1 + y, 1 + z] = jnp.where(amplitude > 0.0, -0.5, 0.0) / jnp.sqrt(level)
        send(slo, e, slo_send, slo_recv)
        for y, z in cells:
            own[2 * y + z, 0] = across_rows(3.0 * slo[e, 1, 1 + y, 1 + z])
        first_forces()
        for c in range(4):
            total[c] = lane_sums(c)
            for k in range(4):
                acc[c, k] = jnp.zeros((128, 128), f32)
        for group in (0, 1, 2, 4, 5):
            wait(slo, e, slo_recv, arrival(group))
            if group == 2:
                wait(slo, e, slo_recv, 3)
            count, line_at = fetched[group]

            def spread(index, carry):
                line = line_at(index)
                ix, iy = line // 4, line % 4
                for iz in range(4):
                    lanes = pl.ds(128 * iz, 128)
                    slope = 3.0 * slo[e, ix, iy, iz]
                    keep(line, 8, lanes, slope)
                    for k in range(3):
                        rows[line, 5 + k, :, lanes] = slope * rows[line, 2 + k, :, lanes]
                return carry

            lax.fori_loop(0, count, spread, 0)
            add_forces(group)
        kick = jnp.where(e == 1, 2.0, 1.0) * (0.5 * time_step)
        for y, z in cells:
            c = 2 * y + z
            tile = ext[e, 1, 1 + y, 1 + z]
            place_ = tile + shift_of(1, 1 + y, 1 + z)
            r = total[c] + tile[3:4] * lane_sums(c)
            force = -2.0 * (r - place_ * r[3:4])
            v = vel[c]
            push = kick * v[3:4] * force
            for k in range(3):
                out_vel[k, y, pl.ds(z, 1)] = v[k : k + 1]
                out_push[k, y, pl.ds(z, 1)] = push[k : k + 1]
            v = jnp.where(row4 < 3, v + push, v)
            vel[c] = v
            ext[e + 1, 1, 1 + y, 1 + z] = jnp.where(row4 < 3, tile + time_step * v, tile)
        return carry

    lax.fori_loop(0, 3, evaluate, 0)
    for y, z in cells:
        for k in range(3):
            out_pos[k, y, pl.ds(z, 1)] = ext[1, 1, 1 + y, 1 + z][k : k + 1]

    def drain(e, carry):
        for group in range(6):
            wait(ext, e, pos_send, group)
            wait(slo, e, slo_send, group)
        return carry

    lax.fori_loop(0, 3, drain, 0)


def on_device(positions, velocities, species, counts):
    vmem = pl.BlockSpec(memory_space=pltpu.VMEM)
    shape = jax.ShapeDtypeStruct((3, 2, 2, 128), f32)
    before, velocity, push = pl.pallas_call(
        kernel,
        out_shape=(shape, shape, shape),
        in_specs=[pl.BlockSpec(memory_space=pltpu.HBM)] * 4,
        out_specs=(vmem, vmem, vmem),
        scratch_shapes=[
            pltpu.VMEM((4, 3, 4, 4, 4, 128), f32),
            pltpu.VMEM((3, 3, 4, 4, 1, 128), f32),
            pltpu.VMEM((12, 32, 512), bf16),
            pltpu.VMEM((12, 9, 8, 512), f32),
            pltpu.VMEM((512, 32), bf16),
            pltpu.VMEM((4, 2, 128, 128), f32),
            pltpu.VMEM((4, 12, 128, 384), f32),
            pltpu.VMEM((4, 4, 128, 128), f32),
            pltpu.VMEM((4, 4, 128), f32),
            pltpu.VMEM((4, 4, 128), f32),
        ]
        + [pltpu.VMEM((3, 2, 2, 128), f32)] * 2
        + [pltpu.VMEM((2, 2, 128), jnp.int32), pltpu.VMEM((2, 2), jnp.int32)]
        + [pltpu.SemaphoreType.DMA((3, 6))] * 4
        + [pltpu.SemaphoreType.DMA((4,))],
        compiler_params=pltpu.CompilerParams(
            collective_id=0, has_side_effects=True, vmem_limit_bytes=32 * 1024 * 1024
        ),
    )(*(pltpu.with_memory_space_constraint(a, pltpu.HBM) for a in (positions[:, 0], velocities[:, 0], species[0], counts[0])))
    return (before + time_step * velocity)[:, None], (velocity + push)[:, None]


def solution(mesh):
    return jax.shard_map(
        on_device,
        mesh=mesh,
        in_specs=(
            P(None, "gx", "gy", "gz", None),
            P(None, "gx", "gy", "gz", None),
            P("gx", "gy", "gz", None),
            P("gx", "gy", "gz"),
        ),
        out_specs=(P(None, "gx", "gy", "gz", None), P(None, "gx", "gy", "gz", None)),
        check_vma=False,
    )
```

```python
import functools
import itertools

import jax
import jax.numpy as jnp
from jax import lax
from jax.experimental import pallas as pl
from jax.experimental.pallas import tpu as pltpu
from jax.sharding import PartitionSpec as P

MESH = pl.DeviceIdType.MESH
time_step = 0.05
AXES = ("gx", "gy", "gz")
SOURCE = {0: (1, 2), 1: (2, 1), -1: (1, 1)}
TARGET = {0: 1, 1: 0, -1: 3}
DIRECTIONS = sorted(
    (d for d in itertools.product((-1, 0, 1), repeat=3) if d != (0, 0, 0)),
    key=lambda d: -(4 * abs(d[0] * d[1]) + 2 * abs(d[0]) + 2 * abs(d[1]) + abs(d[2])),
)
f32, bf16 = jnp.float32, jnp.bfloat16
CHUNK = 64


def group_of(d):
    if d[0] == 0:
        return 0 if d[1] == 0 else 1
    if d[1] == 0:
        return 2 if d[2] == 0 else 3
    return 4 if d[1] == 1 else 5


def group_ref(buffer, group):
    if isinstance(group, int) and group == 0:
        return buffer.at[1, 0]
    return buffer.at[1, pl.ds(0, 2)]


def pieces(value):
    high = value.astype(bf16).astype(f32)
    rest = value - high
    middle = rest.astype(bf16).astype(f32)
    return high, middle, rest - middle


def strength_of(amplitude):
    return jnp.where(amplitude > 1.15, 0.4, jnp.where(amplitude > 0.0, 0.3, 0.0)).astype(f32)


def kernel(
    pos_hbm, vel_hbm, spec_hbm, count_hbm, out_pos, out_vel, out_push,
    ext, slo, part, rows, lhs, own, near, acc, total, vel,
    pos_ref, vel_ref, spec_ref, count_ref, pos_send, pos_recv, slo_send, slo_recv, load_sem,
):
    place = [lax.axis_index(a) for a in AXES]
    sizes = [lax.axis_size(a) for a in AXES]

    def device(d):
        return tuple(lax.rem(m + k + s, k) for m, k, s in zip(place, sizes, d))

    barrier = pltpu.get_barrier_semaphore()
    for d in DIRECTIONS:
        pl.semaphore_signal(barrier, inc=1, device_id=device(d), device_id_type=MESH)

    loads = [
        pltpu.make_async_copy(source, target, load_sem.at[k])
        for k, (source, target) in enumerate(
            [(pos_hbm, pos_ref), (spec_hbm, spec_ref), (count_hbm, count_ref), (vel_hbm, vel_ref)]
        )
    ]
    for load in loads:
        load.start()
    for load in loads:
        load.wait()

    row4 = lax.broadcasted_iota(jnp.int32, (4, 128), 0)
    slot = lax.broadcasted_iota(jnp.int32, (1, 128), 1)
    cells = [(y, z) for y in range(2) for z in range(2)]
    for y, z in cells:
        c = 2 * y + z
        present = slot < count_ref[pl.ds(y, 1), pl.ds(z, 1)]
        species = spec_ref[y, pl.ds(z, 1)]
        amplitude = jnp.where(present, jnp.where(species == 1, 1.3, 1.0), 0.0).astype(f32)
        inverse_mass = jnp.where(species == 1, 1.6, 1.0).astype(f32)
        ext[0, 1, 1 + y, 1 + z] = jnp.concatenate([pos_ref[k, y, pl.ds(z, 1)] for k in range(3)] + [amplitude], axis=0)
        vel[c] = jnp.concatenate([vel_ref[k, y, pl.ds(z, 1)] for k in range(3)] + [inverse_mass], axis=0)

    pl.semaphore_wait(barrier, len(DIRECTIONS))

    last = lax.rem(place[0] + 1, 2)
    side_of = {4: 1 - last, 5: last}

    def copy_out(buffer, e, send_sem, recv_sem, group, source, target, d):
        (sz, nz), tz = SOURCE[d[2]], TARGET[d[2]]
        pltpu.make_async_remote_copy(
            src_ref=buffer.at[e, 1, source, pl.ds(sz, nz)],
            dst_ref=buffer.at[e, 1 - d[0], target, pl.ds(tz, nz)],
            send_sem=send_sem.at[e, group],
            recv_sem=recv_sem.at[e, group],
            device_id=device(d),
            device_id_type=MESH,
        ).start()

    def send_row(y, *where):
        for dx in (-1, 1, 0):
            for dz in (-1, 1, 0):
                group = 5 - y if dx else 1
                copy_out(*where, group, pl.ds(1 + y, 1), pl.ds(3 * (1 - y), 1), (dx, 2 * y - 1, dz))

    def send_level(*where):
        for d in DIRECTIONS:
            if d[1] == 0:
                copy_out(*where, group_of(d), pl.ds(1, 2), pl.ds(1, 2), d)

    def wait(buffer, e, sem, group):
        ref = group_ref(buffer.at[e], group)
        pltpu.make_async_copy(ref, ref, sem.at[e, group]).wait()

    def shift_of(ix, iy, iz):
        fx, fy = (jnp.asarray(v, jnp.int32).astype(f32) for v in (ix, iy))
        return jnp.where(row4 == 0, fx - 1.5, jnp.where(row4 == 1, fy - 2.0, float(iz - 2)))

    def keep(line, k, lanes, value):
        rows[line, k, :, lanes] = jnp.broadcast_to(value, (8, 128))

    def prepare(e, columns, count, line_at):
        def one(index, carry):
            line = line_at(index)
            ix, iy = line // 4, line % 4
            for iz in columns:
                lanes = pl.ds(128 * iz, 128)
                tile = ext[e, ix, iy, iz]
                place_ = tile + shift_of(ix, iy, iz)
                square = jnp.sum(jnp.where(row4 < 3, place_ * place_, 0.0), axis=0, keepdims=True)
                h, m, l = pieces(jnp.where(row4 < 3, place_, square))
                one_ = jnp.ones_like(h)
                zero = jnp.zeros_like(h)
                part[line, :, lanes] = jnp.concatenate([h, m, h, m, l, h, one_, zero], axis=0).astype(bf16)
                amplitude = tile[3:4]
                keep(line, 0, lanes, amplitude)
                keep(line, 1, lanes, 2.0 * strength_of(amplitude))
                for k in range(3):
                    keep(line, 2 + k, lanes, place_[k : k + 1])
            return carry

        lax.fori_loop(0, count, one, 0)

    fetched = {
        0: (2, lambda k: 5 + k),
        1: (2, lambda k: 4 + 3 * k),
        2: (4, lambda k: 8 * (k // 2) + 1 + k % 2),
        4: (2, lambda k: 8 * k + 3 * side_of[4]),
        5: (2, lambda k: 8 * k + 3 * side_of[5]),
    }

    def weighted(s, line, z):
        out = None
        for k in range(s.shape[1] // 128):
            v = fold(s[:, 128 * k : 128 * k + 128])
            v = v * v * (v * rows[line, 0, :, pl.ds(128 * (z + k), 128)])
            out = v if out is None else out + v
        return out.reshape(128, 128)

    def smooth(first, count, line, lanes):
        t = jnp.dot(lhs[pl.ds(first, count)], part[line, :, lanes], preferred_element_type=f32)
        return jnp.maximum(t, 0.0)

    def strips(y, lines):
        for z in range(2):
            total_ = 0.0
            for line in lines:
                s = smooth(pl.multiple_of(256 * z + 128 * y, 128), 128, line, pl.ds(128 * z, 384))
                near[2 * y + z, line] = s
                total_ = total_ + weighted(s, line, z)
            acc[2 * y + z, 0] += total_

    def core(line):
        s = smooth(0, 512, line, pl.ds(128, 256))
        for y, z in cells:
            mine = s[256 * z + 128 * y : 256 * z + 128 * y + 128]
            near[2 * y + z, line, :, pl.ds(128 - 128 * z, 256)] = mine
            acc[2 * y + z, 0] += weighted(mine, line, 1)

    def rim(lines):
        for z in range(2):
            found = [smooth(256 * z, 256, line, pl.ds(384 * z, 128)) for line in lines]
            for y in range(2):
                extra = 0.0
                for line, s in zip(lines, found):
                    mine = s[128 * y : 128 * y + 128]
                    near[2 * y + z, line, :, pl.ds(256 * z, 128)] = mine
                    extra = extra + weighted(mine, line, 3 * z)
                acc[2 * y + z, 0] += extra

    def sweep(count, body):
        def one(index, carry):
            parts = 128 // count
            c = index // parts
            body(c, c // 2, c % 2, pl.ds(pl.multiple_of(count * (index % parts), count), count))
            return carry

        lax.fori_loop(0, 4 * (128 // count), one, 0)

    def tiles(lines, z):
        for line in lines:
            for k in range(3):
                yield line, pl.ds(128 * k, 128), pl.ds(pl.multiple_of(128 * (z + k), 128), 128)

    def fold(value):
        return value.reshape(-1, 8, 128)

    def first_forces():
        def body(c, y, z, chunk):
            slope, strength = fold(own[c, 0, chunk]), fold(own[c, 1, chunk])
            sums = [jnp.zeros(slope.shape, f32) for _ in range(4)]
            for line, at, lanes in tiles([4 * ix + y + k for ix in range(3) for k in range(3)], z):
                s = fold(near[c, line, chunk, at])
                square = s * s
                near[c, line, chunk, at] = square.reshape(-1, 128)
                w = square * (slope * rows[line, 0, :, lanes]) + s * (strength * rows[line, 1, :, lanes])
                sums[3] = sums[3] + w
                for k in range(3):
                    sums[k] = sums[k] + w * rows[line, 2 + k, :, lanes]
            for k in range(4):
                acc[c, k, chunk] = sums[k].reshape(-1, 128)

        sweep(CHUNK, body)

    def add_forces(group):
        def body(c, lines, z):
            sums = [fold(acc[c, k]) for k in range(4)]
            for line, at, lanes in tiles(lines, z):
                square = fold(near[c, line, :, at])
                for k in range(4):
                    sums[k] = sums[k] + square * rows[line, 5 + k, :, lanes]
            for k in range(4):
                acc[c, k] = sums[k].reshape(128, 128)

        def one(c, carry):
            y, z = c // 2, c % 2
            body(c, {0: [5, 6], 1: [4 + 3 * y], 2: [1, 2, 9, 10]}[group], z)
            return carry

        if group < 4:
            lax.fori_loop(0, 4, one, 0)
        else:
            y = side_of[group]
            for z in range(2):
                body(2 * y + z, [3 * y, 8 + 3 * y], z)

    def lane_sums(c):
        return jnp.concatenate([jnp.sum(jnp.transpose(acc[c, k]), axis=0, keepdims=True) for k in range(4)], axis=0)

    def across_rows(value):
        return jnp.transpose(jnp.broadcast_to(value, (128, 128)))

    def arrival(group):
        return group if group < 4 else 4 + side_of[group]

    def advance(e, y, z):
        kick = jnp.where(e == 1, 2.0, 1.0) * (0.5 * time_step)
        c = 2 * y + z
        tile = ext[e, 1, 1 + y, 1 + z]
        place_ = tile + shift_of(1, 1 + y, 1 + z)
        r = total[c] + tile[3:4] * lane_sums(c)
        force = -2.0 * (r - place_ * r[3:4])
        v = vel[c]
        push = kick * v[3:4] * force
        for k in range(3):
            out_vel[k, y, pl.ds(z, 1)] = v[k : k + 1]
            out_push[k, y, pl.ds(z, 1)] = push[k : k + 1]
        v = jnp.where(row4 < 3, v + push, v)
        vel[c] = v
        ext[e + 1, 1, 1 + y, 1 + z] = jnp.where(row4 < 3, tile + time_step * v, tile)

    def evaluate(e, carry):
        for y, z in cells:
            c = 2 * y + z
            place_ = ext[e, 1, 1 + y, 1 + z] + shift_of(1, 1 + y, 1 + z)
            square = jnp.sum(jnp.where(row4 < 3, place_ * place_, 0.0), axis=0, keepdims=True)
            h, m, l = pieces(2.0 * place_)
            th, tm, tl = pieces(1.0 - square)
            end = lambda v, fill: jnp.where(row4 < 3, v, fill)
            ends = jnp.where(row4 == 0, th, jnp.where(row4 == 1, tm, jnp.where(row4 == 2, tl, 0.0)))
            side = jnp.concatenate(
                [end(h, -1.0), end(h, -1.0), end(m, 0.0), end(m, 0.0), end(h, -1.0), end(l, 0.0), ends, jnp.zeros_like(h)],
                axis=0,
            )
            lhs[pl.ds(256 * z + 128 * y, 128)] = jnp.transpose(side).astype(bf16)
            acc[c, 0] = jnp.zeros((128, 128), f32)
            own[c, 1] = across_rows(strength_of(ext[e, 1, 1 + y, 1 + z][3:4]))
        prepare(e, (1, 2), *fetched[0])
        core(5)
        core(6)
        wait(ext, e, pos_recv, 0)
        prepare(e, (0, 3), *fetched[0])
        rim([5, 6])
        wait(ext, e, pos_recv, 2)
        prepare(e, (1, 2), *fetched[2])
        for line in (1, 2, 9, 10):
            core(line)
        wait(ext, e, pos_recv, 3)
        prepare(e, (0, 3), *fetched[2])
        rim([1, 2, 9, 10])
        wait(ext, e, pos_recv, 1)
        prepare(e, range(4), *fetched[1])
        for y in range(2):
            strips(y, [4 + 3 * y])
        for group in (4, 5):
            wait(ext, e, pos_recv, arrival(group))
            prepare(e, range(4), *fetched[group])
            y = side_of[group]
            strips(y, [3 * y, 8 + 3 * y])
            for z in range(2):
                amplitude = ext[e, 1, 1 + y, 1 + z][3:4]
                level = jnp.sum(jnp.transpose(acc[2 * y + z, 0]), axis=0, keepdims=True) - amplitude + 1.0
                slo[e, 1, 1 + y, 1 + z] = jnp.where(amplitude > 0.0, -0.5, 0.0) / jnp.sqrt(level)
            send_row(y, slo, e, slo_send, slo_recv)
        send_level(slo, e, slo_send, slo_recv)
        for y, z in cells:
            own[2 * y + z, 0] = across_rows(3.0 * slo[e, 1, 1 + y, 1 + z])
        first_forces()
        for c in range(4):
            total[c] = lane_sums(c)
            for k in range(4):
                acc[c, k] = jnp.zeros((128, 128), f32)
        for group in (0, 1, 2, 4, 5):
            wait(slo, e, slo_recv, arrival(group))
            if group == 2:
                wait(slo, e, slo_recv, 3)
            count, line_at = fetched[group]

            def spread(index, carry):
                line = line_at(index)
                ix, iy = line // 4, line % 4
                for iz in range(4):
                    lanes = pl.ds(128 * iz, 128)
                    slope = 3.0 * slo[e, ix, iy, iz]
                    keep(line, 8, lanes, slope)
                    for k in range(3):
                        rows[line, 5 + k, :, lanes] = slope * rows[line, 2 + k, :, lanes]
                return carry

            lax.fori_loop(0, count, spread, 0)
            add_forces(group)

            if group < 4:
                continue
            y = side_of[group]
            for z in range(2):
                advance(e, y, z)

            @pl.when(e < 2)
            def _():
                send_row(y, ext, e + 1, pos_send, pos_recv)

        @pl.when(e < 2)
        def _():
            send_level(ext, e + 1, pos_send, pos_recv)

        return carry

    send_row(side_of[5], ext, 0, pos_send, pos_recv)
    send_level(ext, 0, pos_send, pos_recv)
    send_row(side_of[4], ext, 0, pos_send, pos_recv)
    lax.fori_loop(0, 3, evaluate, 0)
    for y, z in cells:
        for k in range(3):
            out_pos[k, y, pl.ds(z, 1)] = ext[1, 1, 1 + y, 1 + z][k : k + 1]

    def drain(e, carry):
        for group in range(6):
            wait(ext, e, pos_send, group)
            wait(slo, e, slo_send, group)
        return carry

    lax.fori_loop(0, 3, drain, 0)


def on_device(positions, velocities, species, counts):
    vmem = pl.BlockSpec(memory_space=pltpu.VMEM)
    shape = jax.ShapeDtypeStruct((3, 2, 2, 128), f32)
    before, velocity, push = pl.pallas_call(
        kernel,
        out_shape=(shape, shape, shape),
        in_specs=[pl.BlockSpec(memory_space=pltpu.HBM)] * 4,
        out_specs=(vmem, vmem, vmem),
        scratch_shapes=[
            pltpu.VMEM((4, 3, 4, 4, 4, 128), f32),
            pltpu.VMEM((3, 3, 4, 4, 1, 128), f32),
            pltpu.VMEM((12, 32, 512), bf16),
            pltpu.VMEM((12, 9, 8, 512), f32),
            pltpu.VMEM((512, 32), bf16),
            pltpu.VMEM((4, 2, 128, 128), f32),
            pltpu.VMEM((4, 12, 128, 384), f32),
            pltpu.VMEM((4, 4, 128, 128), f32),
            pltpu.VMEM((4, 4, 128), f32),
            pltpu.VMEM((4, 4, 128), f32),
        ]
        + [pltpu.VMEM((3, 2, 2, 128), f32)] * 2
        + [pltpu.VMEM((2, 2, 128), jnp.int32), pltpu.VMEM((2, 2), jnp.int32)]
        + [pltpu.SemaphoreType.DMA((3, 6))] * 4
        + [pltpu.SemaphoreType.DMA((4,))],
        compiler_params=pltpu.CompilerParams(
            collective_id=0, has_side_effects=True, vmem_limit_bytes=32 * 1024 * 1024
        ),
    )(*(pltpu.with_memory_space_constraint(a, pltpu.HBM) for a in (positions[:, 0], velocities[:, 0], species[0], counts[0])))
    return (before + time_step * velocity)[:, None], (velocity + push)[:, None]


def solution(mesh):
    return jax.shard_map(
        on_device,
        mesh=mesh,
        in_specs=(
            P(None, "gx", "gy", "gz", None),
            P(None, "gx", "gy", "gz", None),
            P("gx", "gy", "gz", None),
            P("gx", "gy", "gz"),
        ),
        out_specs=(P(None, "gx", "gy", "gz", None), P(None, "gx", "gy", "gz", None)),
        check_vma=False,
    )
```

```python
import functools
import itertools

import jax
import jax.numpy as jnp
from jax import lax
from jax.experimental import pallas as pl
from jax.experimental.pallas import tpu as pltpu
from jax.sharding import PartitionSpec as P

MESH = pl.DeviceIdType.MESH
time_step = 0.05
AXES = ("gx", "gy", "gz")
SOURCE = {0: (1, 2), 1: (2, 1), -1: (1, 1)}
TARGET = {0: 1, 1: 0, -1: 3}
DIRECTIONS = sorted(
    (d for d in itertools.product((-1, 0, 1), repeat=3) if d != (0, 0, 0)),
    key=lambda d: -(4 * abs(d[0] * d[1]) + 2 * abs(d[0]) + 2 * abs(d[1]) + abs(d[2])),
)
f32, bf16 = jnp.float32, jnp.bfloat16
CHUNK = 64


def group_of(d):
    if d[0] == 0:
        return 0 if d[1] == 0 else 1
    if d[1] == 0:
        return 2 if d[2] == 0 else 3
    return 4 if d[1] == 1 else 5


def group_ref(buffer, group):
    if isinstance(group, int) and group == 0:
        return buffer.at[1, 0]
    return buffer.at[1, pl.ds(0, 2)]


def pieces(value):
    high = value.astype(bf16).astype(f32)
    rest = value - high
    middle = rest.astype(bf16).astype(f32)
    return high, middle, rest - middle


def strength_of(amplitude):
    return jnp.where(amplitude > 1.15, 0.4, jnp.where(amplitude > 0.0, 0.3, 0.0)).astype(f32)


def kernel(
    pos_hbm, vel_hbm, spec_hbm, count_hbm, out_pos, out_vel, out_push,
    ext, slo, part, rows, lhs, own, near, acc, total, vel,
    pos_ref, vel_ref, spec_ref, count_ref, pos_send, pos_recv, slo_send, slo_recv, load_sem,
):
    place = [lax.axis_index(a) for a in AXES]
    sizes = [lax.axis_size(a) for a in AXES]

    def device(d):
        return tuple(lax.rem(m + k + s, k) for m, k, s in zip(place, sizes, d))

    barrier = pltpu.get_barrier_semaphore()
    for d in DIRECTIONS:
        pl.semaphore_signal(barrier, inc=1, device_id=device(d), device_id_type=MESH)

    loads = [
        pltpu.make_async_copy(source, target, load_sem.at[k])
        for k, (source, target) in enumerate(
            [(pos_hbm, pos_ref), (spec_hbm, spec_ref), (count_hbm, count_ref), (vel_hbm, vel_ref)]
        )
    ]
    for load in loads:
        load.start()
    for load in loads:
        load.wait()

    row4 = lax.broadcasted_iota(jnp.int32, (4, 128), 0)
    slot = lax.broadcasted_iota(jnp.int32, (1, 128), 1)
    cells = [(y, z) for y in range(2) for z in range(2)]
    for y, z in cells:
        c = 2 * y + z
        present = slot < count_ref[pl.ds(y, 1), pl.ds(z, 1)]
        species = spec_ref[y, pl.ds(z, 1)]
        amplitude = jnp.where(present, jnp.where(species == 1, 1.3, 1.0), 0.0).astype(f32)
        inverse_mass = jnp.where(species == 1, 1.6, 1.0).astype(f32)
        ext[0, 1, 1 + y, 1 + z] = jnp.concatenate([pos_ref[k, y, pl.ds(z, 1)] for k in range(3)] + [amplitude], axis=0)
        vel[c] = jnp.concatenate([vel_ref[k, y, pl.ds(z, 1)] for k in range(3)] + [inverse_mass], axis=0)

    pl.semaphore_wait(barrier, len(DIRECTIONS))

    last = lax.rem(place[0] + 1, 2)
    side_of = {4: 1 - last, 5: last}

    def copy_out(buffer, e, send_sem, recv_sem, group, source, target, d):
        (sz, nz), tz = SOURCE[d[2]], TARGET[d[2]]
        pltpu.make_async_remote_copy(
            src_ref=buffer.at[e, 1, source, pl.ds(sz, nz)],
            dst_ref=buffer.at[e, 1 - d[0], target, pl.ds(tz, nz)],
            send_sem=send_sem.at[e, group],
            recv_sem=recv_sem.at[e, group],
            device_id=device(d),
            device_id_type=MESH,
        ).start()

    def send_row(y, *where):
        for dx in (-1, 1, 0):
            for dz in (-1, 1, 0):
                group = 5 - y if dx else 1
                copy_out(*where, group, pl.ds(1 + y, 1), pl.ds(3 * (1 - y), 1), (dx, 2 * y - 1, dz))

    def send_level(*where):
        for d in DIRECTIONS:
            if d[1] == 0:
                copy_out(*where, group_of(d), pl.ds(1, 2), pl.ds(1, 2), d)

    def wait(buffer, e, sem, group):
        ref = group_ref(buffer.at[e], group)
        pltpu.make_async_copy(ref, ref, sem.at[e, group]).wait()

    def shift_of(ix, iy, iz):
        fx, fy = (jnp.asarray(v, jnp.int32).astype(f32) for v in (ix, iy))
        return jnp.where(row4 == 0, fx - 1.5, jnp.where(row4 == 1, fy - 2.0, float(iz - 2)))

    def keep(line, k, lanes, value):
        rows[line, k, :, lanes] = jnp.broadcast_to(value, (8, 128))

    def prepare(e, columns, count, line_at):
        def one(index, carry):
            line = line_at(index)
            ix, iy = line // 4, line % 4
            for iz in columns:
                lanes = pl.ds(128 * iz, 128)
                tile = ext[e, ix, iy, iz]
                place_ = tile + shift_of(ix, iy, iz)
                square = jnp.sum(jnp.where(row4 < 3, place_ * place_, 0.0), axis=0, keepdims=True)
                h, m, l = pieces(jnp.where(row4 < 3, place_, square))
                one_ = jnp.ones_like(h)
                zero = jnp.zeros_like(h)
                part[line, :, lanes] = jnp.concatenate([h, m, h, m, l, h, one_, zero], axis=0).astype(bf16)
                amplitude = tile[3:4]
                keep(line, 0, lanes, amplitude)
                keep(line, 1, lanes, 2.0 * strength_of(amplitude))
                for k in range(3):
                    keep(line, 2 + k, lanes, place_[k : k + 1])
            return carry

        lax.fori_loop(0, count, one, 0)

    fetched = {
        0: (2, lambda k: 5 + k),
        1: (2, lambda k: 4 + 3 * k),
        2: (4, lambda k: 8 * (k // 2) + 1 + k % 2),
        4: (2, lambda k: 8 * k + 3 * side_of[4]),
        5: (2, lambda k: 8 * k + 3 * side_of[5]),
    }

    def weighted(s, line, z):
        out = None
        for k in range(s.shape[1] // 128):
            v = fold(s[:, 128 * k : 128 * k + 128])
            v = v * v * (v * rows[line, 0, :, pl.ds(128 * (z + k), 128)])
            out = v if out is None else out + v
        return out.reshape(128, 128)

    def smooth(first, count, line, lanes):
        t = jnp.dot(lhs[pl.ds(first, count)], part[line, :, lanes], preferred_element_type=f32)
        return jnp.maximum(t, 0.0)

    def strips(y, lines):
        for z in range(2):
            total_ = 0.0
            for line in lines:
                s = smooth(pl.multiple_of(256 * z + 128 * y, 128), 128, line, pl.ds(128 * z, 384))
                near[2 * y + z, line] = s
                total_ = total_ + weighted(s, line, z)
            acc[2 * y + z, 0] += total_

    def core(line):
        s = smooth(0, 512, line, pl.ds(128, 256))
        for y, z in cells:
            mine = s[256 * z + 128 * y : 256 * z + 128 * y + 128]
            near[2 * y + z, line, :, pl.ds(128 - 128 * z, 256)] = mine
            acc[2 * y + z, 0] += weighted(mine, line, 1)

    def rim(lines):
        for z in range(2):
            found = [smooth(256 * z, 256, line, pl.ds(384 * z, 128)) for line in lines]
            for y in range(2):
                extra = 0.0
                for line, s in zip(lines, found):
                    mine = s[128 * y : 128 * y + 128]
                    near[2 * y + z, line, :, pl.ds(256 * z, 128)] = mine
                    extra = extra + weighted(mine, line, 3 * z)
                acc[2 * y + z, 0] += extra

    def sweep(count, body):
        def one(index, carry):
            parts = 128 // count
            c = index // parts
            body(c, c // 2, c % 2, pl.ds(pl.multiple_of(count * (index % parts), count), count))
            return carry

        lax.fori_loop(0, 4 * (128 // count), one, 0)

    def tiles(lines, z):
        for line in lines:
            for k in range(3):
                yield line, pl.ds(128 * k, 128), pl.ds(pl.multiple_of(128 * (z + k), 128), 128)

    def fold(value):
        return value.reshape(-1, 8, 128)

    def outer(z):
        return pl.ds(pl.multiple_of(256 * z, 128), 128), pl.ds(pl.multiple_of(384 * z, 128), 128)

    def first_forces():
        def body(c, y, z, chunk):
            slope, strength, amplitude = (fold(own[c, k, chunk]) for k in range(3))
            sums = [jnp.zeros(slope.shape, f32) for _ in range(4)]

            def add(line, at, lanes, known):
                s = fold(near[c, line, chunk, at])
                square = s * s
                pull = slope * rows[line, 0, :, lanes]
                if known:
                    pull = pull + amplitude * rows[line, 8, :, lanes]
                else:
                    near[c, line, chunk, at] = square.reshape(-1, 128)
                w = square * pull + s * (strength * rows[line, 1, :, lanes])
                sums[3] = sums[3] + w
                for k in range(3):
                    sums[k] = sums[k] + w * rows[line, 2 + k, :, lanes]

            for line in (5, 6):
                for column in (1, 2):
                    add(line, pl.ds(pl.multiple_of(128 * (column - z), 128), 128), pl.ds(128 * column, 128), True)
                add(line, *outer(z), False)
            for tile in tiles([4 + 3 * y] + [4 * ix + y + k for ix in (0, 2) for k in range(3)], z):
                add(*tile, False)
            for k in range(4):
                acc[c, k, chunk] = sums[k].reshape(-1, 128)

        sweep(CHUNK, body)

    def add_forces(group):
        def body(c, lines, z):
            sums = [fold(acc[c, k]) for k in range(4)]
            for line, at, lanes in [(line, *outer(z)) for line in lines] if group == 0 else tiles(lines, z):
                square = fold(near[c, line, :, at])
                for k in range(4):
                    sums[k] = sums[k] + square * rows[line, 5 + k, :, lanes]
            for k in range(4):
                acc[c, k] = sums[k].reshape(128, 128)

        def one(c, carry):
            y, z = c // 2, c % 2
            body(c, {0: [5, 6], 1: [4 + 3 * y], 2: [1, 2, 9, 10]}[group], z)
            return carry

        if group < 4:
            lax.fori_loop(0, 4, one, 0)
        else:
            y = side_of[group]
            for z in range(2):
                body(2 * y + z, [3 * y, 8 + 3 * y], z)

    def lane_sums(c):
        return jnp.concatenate([jnp.sum(jnp.transpose(acc[c, k]), axis=0, keepdims=True) for k in range(4)], axis=0)

    def across_rows(value):
        return jnp.transpose(jnp.broadcast_to(value, (128, 128)))

    def arrival(group):
        return group if group < 4 else 4 + side_of[group]

    def advance(e, y, z):
        kick = jnp.where(e == 1, 2.0, 1.0) * (0.5 * time_step)
        c = 2 * y + z
        tile = ext[e, 1, 1 + y, 1 + z]
        place_ = tile + shift_of(1, 1 + y, 1 + z)
        r = total[c] + tile[3:4] * lane_sums(c)
        force = -2.0 * (r - place_ * r[3:4])
        v = vel[c]
        push = kick * v[3:4] * force
        for k in range(3):
            out_vel[k, y, pl.ds(z, 1)] = v[k : k + 1]
            out_push[k, y, pl.ds(z, 1)] = push[k : k + 1]
        v = jnp.where(row4 < 3, v + push, v)
        vel[c] = v
        ext[e + 1, 1, 1 + y, 1 + z] = jnp.where(row4 < 3, tile + time_step * v, tile)

    def evaluate(e, carry):
        for y, z in cells:
            c = 2 * y + z
            place_ = ext[e, 1, 1 + y, 1 + z] + shift_of(1, 1 + y, 1 + z)
            square = jnp.sum(jnp.where(row4 < 3, place_ * place_, 0.0), axis=0, keepdims=True)
            h, m, l = pieces(2.0 * place_)
            th, tm, tl = pieces(1.0 - square)
            end = lambda v, fill: jnp.where(row4 < 3, v, fill)
            ends = jnp.where(row4 == 0, th, jnp.where(row4 == 1, tm, jnp.where(row4 == 2, tl, 0.0)))
            side = jnp.concatenate(
                [end(h, -1.0), end(h, -1.0), end(m, 0.0), end(m, 0.0), end(h, -1.0), end(l, 0.0), ends, jnp.zeros_like(h)],
                axis=0,
            )
            lhs[pl.ds(256 * z + 128 * y, 128)] = jnp.transpose(side).astype(bf16)
            acc[c, 0] = jnp.zeros((128, 128), f32)
            own[c, 1] = across_rows(strength_of(ext[e, 1, 1 + y, 1 + z][3:4]))
            own[c, 2] = across_rows(ext[e, 1, 1 + y, 1 + z][3:4])
        prepare(e, (1, 2), *fetched[0])
        core(5)
        core(6)
        wait(ext, e, pos_recv, 0)
        prepare(e, (0, 3), *fetched[0])
        rim([5, 6])
        wait(ext, e, pos_recv, 2)
        prepare(e, (1, 2), *fetched[2])
        for line in (1, 2, 9, 10):
            core(line)
        wait(ext, e, pos_recv, 3)
        prepare(e, (0, 3), *fetched[2])
        rim([1, 2, 9, 10])
        wait(ext, e, pos_recv, 1)
        prepare(e, range(4), *fetched[1])
        for y in range(2):
            strips(y, [4 + 3 * y])
        for group in (4, 5):
            wait(ext, e, pos_recv, arrival(group))
            prepare(e, range(4), *fetched[group])
            y = side_of[group]
            strips(y, [3 * y, 8 + 3 * y])
            for z in range(2):
                amplitude = ext[e, 1, 1 + y, 1 + z][3:4]
                level = jnp.sum(jnp.transpose(acc[2 * y + z, 0]), axis=0, keepdims=True) - amplitude + 1.0
                slo[e, 1, 1 + y, 1 + z] = jnp.where(amplitude > 0.0, -0.5, 0.0) / jnp.sqrt(level)
            send_row(y, slo, e, slo_send, slo_recv)
        send_level(slo, e, slo_send, slo_recv)
        for y, z in cells:
            own[2 * y + z, 0] = across_rows(3.0 * slo[e, 1, 1 + y, 1 + z])
            keep(5 + y, 8, pl.ds(128 + 128 * z, 128), 3.0 * slo[e, 1, 1 + y, 1 + z])
        first_forces()
        for c in range(4):
            total[c] = lane_sums(c)
            for k in range(4):
                acc[c, k] = jnp.zeros((128, 128), f32)
        for group in (0, 1, 2, 4, 5):
            wait(slo, e, slo_recv, arrival(group))
            if group == 2:
                wait(slo, e, slo_recv, 3)
            count, line_at = fetched[group]

            def spread(index, carry):
                line = line_at(index)
                ix, iy = line // 4, line % 4
                for iz in range(4):
                    lanes = pl.ds(128 * iz, 128)
                    slope = 3.0 * slo[e, ix, iy, iz]
                    keep(line, 8, lanes, slope)
                    for k in range(3):
                        rows[line, 5 + k, :, lanes] = slope * rows[line, 2 + k, :, lanes]
                return carry

            lax.fori_loop(0, count, spread, 0)
            add_forces(group)

            if group < 4:
                continue
            y = side_of[group]
            for z in range(2):
                advance(e, y, z)

            @pl.when(e < 2)
            def _():
                send_row(y, ext, e + 1, pos_send, pos_recv)

        @pl.when(e < 2)
        def _():
            send_level(ext, e + 1, pos_send, pos_recv)

        return carry

    send_row(side_of[5], ext, 0, pos_send, pos_recv)
    send_level(ext, 0, pos_send, pos_recv)
    send_row(side_of[4], ext, 0, pos_send, pos_recv)
    lax.fori_loop(0, 3, evaluate, 0)
    for y, z in cells:
        for k in range(3):
            out_pos[k, y, pl.ds(z, 1)] = ext[1, 1, 1 + y, 1 + z][k : k + 1]

    def drain(e, carry):
        for group in range(6):
            wait(ext, e, pos_send, group)
            wait(slo, e, slo_send, group)
        return carry

    lax.fori_loop(0, 3, drain, 0)


def on_device(positions, velocities, species, counts):
    vmem = pl.BlockSpec(memory_space=pltpu.VMEM)
    shape = jax.ShapeDtypeStruct((3, 2, 2, 128), f32)
    before, velocity, push = pl.pallas_call(
        kernel,
        out_shape=(shape, shape, shape),
        in_specs=[pl.BlockSpec(memory_space=pltpu.HBM)] * 4,
        out_specs=(vmem, vmem, vmem),
        scratch_shapes=[
            pltpu.VMEM((4, 3, 4, 4, 4, 128), f32),
            pltpu.VMEM((3, 3, 4, 4, 1, 128), f32),
            pltpu.VMEM((12, 32, 512), bf16),
            pltpu.VMEM((12, 9, 8, 512), f32),
            pltpu.VMEM((512, 32), bf16),
            pltpu.VMEM((4, 3, 128, 128), f32),
            pltpu.VMEM((4, 12, 128, 384), f32),
            pltpu.VMEM((4, 4, 128, 128), f32),
            pltpu.VMEM((4, 4, 128), f32),
            pltpu.VMEM((4, 4, 128), f32),
        ]
        + [pltpu.VMEM((3, 2, 2, 128), f32)] * 2
        + [pltpu.VMEM((2, 2, 128), jnp.int32), pltpu.VMEM((2, 2), jnp.int32)]
        + [pltpu.SemaphoreType.DMA((3, 6))] * 4
        + [pltpu.SemaphoreType.DMA((4,))],
        compiler_params=pltpu.CompilerParams(
            collective_id=0, has_side_effects=True, vmem_limit_bytes=32 * 1024 * 1024
        ),
    )(*(pltpu.with_memory_space_constraint(a, pltpu.HBM) for a in (positions[:, 0], velocities[:, 0], species[0], counts[0])))
    return (before + time_step * velocity)[:, None], (velocity + push)[:, None]


def solution(mesh):
    return jax.shard_map(
        on_device,
        mesh=mesh,
        in_specs=(
            P(None, "gx", "gy", "gz", None),
            P(None, "gx", "gy", "gz", None),
            P("gx", "gy", "gz", None),
            P("gx", "gy", "gz"),
        ),
        out_specs=(P(None, "gx", "gy", "gz", None), P(None, "gx", "gy", "gz", None)),
        check_vma=False,
    )
```
